128 devices in a mesh: dp: 8 (over z, y_lo), mp: 16 (over y_hi, x, core).
Axes of the slice: x: 4, y: 4 (y_hi: 2, y_lo: 2; y = y_hi * 2 + y_lo), z: 4, core: 2. Of those that a mesh axis runs over, the one named last changes fastest.
Arguments:
- edge_feats: bfloat16 [32768, 3072], P(('dp', 'mp')), may hold values from -6 to 6
- targets: int32 [32768], P(('dp', 'mp')), may hold values from 0 to 127
- roll_ids: int32 [32768], P(('dp', 'mp')), may hold values from 0 to 63
- counts: int32 [128], P(('dp', 'mp')), may hold values from 32 to 256, as said below
- coefs: float32 [8, 16], replicated, may hold values from 0.05 to 0.45
- weights: bfloat16 [16, 1536, 2, 1536], P(None, 'mp'), may hold values from -0.109375 to 0.109375
- roll_angles: float32 [64], replicated, may hold values from -3.140625 to 3.140625
- atom_cot: bfloat16 [1024, 3072], P(('dp', 'mp')), may hold values from -16 to 16
Outputs:
- atom_out: bfloat16 [1024, 3072], P(('dp', 'mp'))
- edge_grad: bfloat16 [32768, 3072], P(('dp', 'mp'))
- weight_grad: bfloat16 [16, 1536, 2, 1536], P(None, 'mp')
- coef_grad: float32 [8, 16], P('dp')
The draws below stay inside these ranges and needn't reach their ends.
Inputs may be any that keep to these rules, and one draw needn't show every extreme that they name: `counts`: some device uses all 256 slots in every draw.
All inputs are finite; a program needn't handle non-finite values.
Results may differ from the reference program's by a relative error of at most 0.023.
Values may be sent and summed in bfloat16 or wider, within the bound.
A program may use at most 128 MiB of HBM per device.

```python
import jax
import jax.numpy as jnp
from jax import lax

C = 256
NL = 6
EXPERTS = 16
NROLL = 64
SLOTS = 256
ATOM_DEV = 8
K = 1536
ATOMS = 128
EDGES = 32768
N_DP = 8
N_MP = 16
DEVICES = 128


def draw_counts(key, part):
    key = jax.random.fold_in(key, 11)
    first_key, second_key = jax.random.split(key)
    base = jax.random.randint(first_key, (DEVICES,), SLOTS // 8, SLOTS + 1)
    fullest = jax.random.randint(second_key, (), 0, DEVICES)
    return jnp.where(jnp.arange(DEVICES) == fullest, SLOTS, base).astype(jnp.int32)


def touch_ends(array, rng, smallest, top_value):
    extent = array.shape
    index_at = [jax.random.randint(jax.random.fold_in(rng, axis), (), 0, extent[axis]) for axis in range(len(extent))]
    array = array.at[tuple(index_at)].set(smallest)
    longest = extent.index(max(extent))
    index_at[longest] = (index_at[longest] + 1) % extent[longest]
    return array.at[tuple(index_at)].set(top_value)


def block_levels(key, dims, shards, low, largest):
    gain = 1.0
    for dim, shards_of in shards:
        draws = jax.random.uniform(jax.random.fold_in(jax.random.fold_in(key, 6), dim), (shards_of,), jnp.float32, low / len(shards), largest / len(shards))
        gain = gain * jnp.repeat(jnp.exp(draws), dims[dim] // shards_of).reshape((-1,) + (1,) * (len(dims) - 1 - dim))
    return gain


def bell_draw(key, dims, scale, reach, shards=(), kind=jnp.bfloat16):
    level = block_levels(key, dims, shards, -0.22, 0.18) if shards else 1.0
    array = jax.random.normal(key, dims, jnp.float32) * scale * level
    return jnp.minimum(jnp.maximum(array, -reach), reach).astype(kind)


def setup_inputs(seed: int = 0) -> dict:
    streams_of = jax.random.split(jax.random.key(seed), 9)
    edge_feats = bell_draw(streams_of[0], (EDGES, 2 * K), 1.0, 6.0, ((0, 128),))
    targets = touch_ends(jax.random.randint(streams_of[1], (EDGES,), 0, ATOMS), jax.random.fold_in(streams_of[1], 1), 0, ATOMS - 1).astype(jnp.int32)
    roll_ids = touch_ends(jax.random.randint(streams_of[2], (EDGES,), 0, NROLL), jax.random.fold_in(streams_of[2], 1), 0, NROLL - 1).astype(jnp.int32)
    counts = draw_counts(jax.random.fold_in(streams_of[8], 71), 0)
    coefs = jnp.clip(jax.random.uniform(streams_of[4], (N_DP, EXPERTS), jnp.float32, 0.05, 0.45), 0.05, 0.45)
    weights = bell_draw(streams_of[5], (EXPERTS, K, 2, K), (2 * K) ** -0.5, 0.109375, ((1, 16),))
    roll_angles = jnp.clip(jax.random.uniform(streams_of[6], (NROLL,), jnp.float32, -3.140625, 3.140625), -3.140625, 3.140625)
    atom_cot = bell_draw(streams_of[7], (N_DP * ATOMS, 2 * K), 4.0, 16.0, ((0, 128),))
    return {"edge_feats": edge_feats, "targets": targets, "roll_ids": roll_ids, "counts": counts, "coefs": coefs, "weights": weights, "roll_angles": roll_angles, "atom_cot": atom_cot}


def reference(edge_feats, targets, roll_ids, counts, coefs, weights, roll_angles, atom_cot):
    highest = lax.Precision.HIGHEST
    width = NL * C
    group_size = SLOTS * N_MP
    scale = (ATOM_DEV / SLOTS) ** 0.5
    grad_norm = (SLOTS * N_MP) ** -0.5
    positions = jnp.arange(SLOTS * N_DP * N_MP, dtype=jnp.int32)
    device_of = positions // SLOTS
    valid = ((positions % SLOTS) < counts[device_of]).astype(jnp.float32)[:, None]
    angles = roll_angles[roll_ids][:, None]
    cosine_all, sine_all = jnp.cos(angles), jnp.sin(angles)
    weights_wide = weights.astype(jnp.float32)
    weight_sum = jnp.zeros(weights.shape, jnp.float32)
    atom_blocks, edge_blocks, coef_rows = [], [], []
    for crystal in range(N_DP):
        lower, upper = crystal * group_size, (crystal + 1) * group_size
        merged = jnp.einsum("k,krab->rab", coefs[crystal], weights_wide, precision=highest).astype(jnp.bfloat16)
        real_part, imag_part = merged[:, 0, :], merged[:, 1, :]
        feats = edge_feats[lower:upper]
        plus_in, minus_in = feats[:, :width], feats[:, width:]
        out_plus = jnp.dot(plus_in, real_part, preferred_element_type=jnp.float32) - jnp.dot(minus_in, imag_part, preferred_element_type=jnp.float32)
        out_minus = jnp.dot(plus_in, imag_part, preferred_element_type=jnp.float32) + jnp.dot(minus_in, real_part, preferred_element_type=jnp.float32)
        factor = scale * valid[lower:upper]
        cosine, sine = cosine_all[lower:upper], sine_all[lower:upper]
        rolled = jnp.concatenate([(cosine * out_plus - sine * out_minus) * factor, (sine * out_plus + cosine * out_minus) * factor], 1)
        onehot = (targets[lower:upper][:, None] == jnp.arange(ATOMS, dtype=jnp.int32)[None, :]).astype(jnp.float32)
        atom_blocks.append(jnp.dot(onehot.T, rolled, precision=highest).astype(jnp.bfloat16))
        cot_block = atom_cot[crystal * ATOMS:(crystal + 1) * ATOMS].astype(jnp.float32)
        cot_edges = jnp.dot(onehot, cot_block, precision=highest) * factor
        cot_plus, cot_minus = cot_edges[:, :width], cot_edges[:, width:]
        grad_plus = (cosine * cot_plus + sine * cot_minus).astype(jnp.bfloat16)
        grad_minus = (cosine * cot_minus - sine * cot_plus).astype(jnp.bfloat16)
        back_plus = jnp.dot(grad_plus, real_part.T, preferred_element_type=jnp.float32) + jnp.dot(grad_minus, imag_part.T, preferred_element_type=jnp.float32)
        back_minus = jnp.dot(grad_minus, real_part.T, preferred_element_type=jnp.float32) - jnp.dot(grad_plus, imag_part.T, preferred_element_type=jnp.float32)
        edge_blocks.append(jnp.concatenate([back_plus, back_minus], 1).astype(jnp.bfloat16))
        grad_merged = jnp.zeros((width, 2, width), jnp.float32)
        for member in range(N_MP):
            first, last = member * SLOTS, (member + 1) * SLOTS
            plus_cols, minus_cols = plus_in[first:last].T, minus_in[first:last].T
            d_real = jnp.dot(plus_cols, grad_plus[first:last], preferred_element_type=jnp.float32) + jnp.dot(minus_cols, grad_minus[first:last], preferred_element_type=jnp.float32)
            d_imag = jnp.dot(plus_cols, grad_minus[first:last], preferred_element_type=jnp.float32) - jnp.dot(minus_cols, grad_plus[first:last], preferred_element_type=jnp.float32)
            rounded = (jnp.stack([d_real, d_imag], 1) * grad_norm).astype(jnp.bfloat16)
            grad_merged = grad_merged + lax.optimization_barrier(rounded).astype(jnp.float32)
        weight_sum = weight_sum + coefs[crystal][:, None, None, None] * grad_merged[None]
        coef_rows.append(jnp.einsum("krab,rab->k", weights_wide, grad_merged, precision=highest) / width ** 0.5)
    return (jnp.concatenate(atom_blocks, 0), jnp.concatenate(edge_blocks, 0), weight_sum.astype(jnp.bfloat16), jnp.stack(coef_rows, 0))
```

```python
import functools

import jax
import jax.numpy as jnp
from jax import lax
from jax.experimental import pallas as pl
from jax.experimental.pallas import tpu as pltpu
from jax.sharding import PartitionSpec as P

BF16, F32 = jnp.bfloat16, jnp.float32
LANES = 128


def dot(a, b, contract):
    return lax.dot_general(a, b, (contract, ((), ())), preferred_element_type=F32)


def turn(rows):
    n = rows.shape[1]
    col = lax.broadcasted_iota(jnp.int32, rows.shape, 1)
    return jnp.where(col // 8 % 2 == 0, jnp.roll(rows, -8, 1), -jnp.roll(rows, 8, 1))


def mix_kernel(experts, crystals, norm, steps, coefs_ref, x_ref, cot_ref, back_ref, spread_ref, wg_ref, eg_ref,
               gm_ref, flat_ref, left_ref):
    step = pl.program_id(0)
    rows = x_ref.shape[1]
    width = cot_ref.shape[2]
    tiles = width // LANES

    @pl.when(step == 0)
    def _():
        r = lax.broadcasted_iota(jnp.int32, (16 * experts, 16 * crystals), 0)
        c = lax.broadcasted_iota(jnp.int32, (16 * experts, 16 * crystals), 1)
        mixed = jnp.zeros((16 * experts, 16 * crystals), F32)
        for k in range(experts):
            for i in range(crystals):
                mixed = jnp.where((r // 16 == k) & (c // 16 == i), coefs_ref[i, k], mixed)
        mixed = jnp.where(r % 16 == c % 16, mixed, 0.0)
        high = mixed.astype(BF16)
        left_ref[:, : 16 * crystals] = high
        left_ref[:, 16 * crystals :] = (mixed - high.astype(F32)).astype(BF16)
        for i in range(crystals):
            x = x_ref[i].astype(F32)
            both = jnp.concatenate([x, -turn(x)], 0).astype(BF16)
            for t in range(tiles):
                grad = dot(both, cot_ref[i, :, t * LANES : (t + 1) * LANES], ((1,), (0,))) * norm
                for part in range(2):
                    flat_ref[pl.ds(t * 2 + part, rows, stride=2 * tiles), :] = grad[part * rows : (part + 1) * rows]
            gm_ref[i] = flat_ref[...].astype(BF16)

    chunk = wg_ref.shape[1]
    for pair in range(chunk // 32):
        start = pl.multiple_of(step * chunk + pair * 32, 32)
        first = [gm_ref[i, pl.ds(start, 16), :] for i in range(crystals)]
        second = [gm_ref[i, pl.ds(start + 16, 16), :] for i in range(crystals)]
        right = jnp.concatenate([jnp.concatenate(first * 2, 0), jnp.concatenate(second * 2, 0)], 1)
        out = dot(left_ref[...], right, ((1,), (0,))).astype(BF16)
        for k in range(experts):
            wg_ref[k, pair * 32 : pair * 32 + 16, :] = out[k * 16 : (k + 1) * 16, :LANES]
            wg_ref[k, pair * 32 + 16 : pair * 32 + 32, :] = out[k * 16 : (k + 1) * 16, LANES:]
    part = step // (steps // 2)
    cols = eg_ref.shape[1]
    at = pl.multiple_of(step % (steps // 2) * cols, cols)
    eg_ref[...] = dot(spread_ref[part], back_ref[pl.ds(at, cols), :], ((1,), (1,))).astype(BF16)


def mix(coefs, x_all, cot_all, back_all, spread, norm):
    crystals, experts = coefs.shape
    _, rows, q = x_all.shape
    width = cot_all.shape[2]
    flat = rows * 2 * width // LANES
    slots = spread.shape[1]
    steps = 12
    whole = lambda shape: pl.BlockSpec(shape, lambda i: (0,) * len(shape))
    return pl.pallas_call(
        functools.partial(mix_kernel, experts, crystals, norm, steps),
        grid=(steps,),
        in_specs=[
            pl.BlockSpec(memory_space=pltpu.SMEM),
            whole(x_all.shape),
            whole(cot_all.shape),
            whole(back_all.shape),
            whole(spread.shape),
        ],
        out_specs=[
            pl.BlockSpec((experts, flat // steps, LANES), lambda i: (0, i, 0)),
            pl.BlockSpec((slots, 2 * width // steps), lambda i: (0, i)),
        ],
        out_shape=[
            jax.ShapeDtypeStruct((experts, flat, LANES), BF16),
            jax.ShapeDtypeStruct((slots, 2 * width), BF16),
        ],
        scratch_shapes=[
            pltpu.VMEM((crystals, flat, LANES), BF16),
            pltpu.VMEM((flat, LANES), F32),
            pltpu.VMEM((16 * experts, 32 * crystals), BF16),
        ],
        compiler_params=pltpu.CompilerParams(vmem_limit_bytes=48 * 2**20),
        cost_estimate=pl.CostEstimate(flops=10**10, bytes_accessed=2 * 10**7, transcendentals=0),
    )(coefs, x_all, cot_all, back_all, spread)


def on_device(edge_feats, targets, roll_ids, counts, coefs, weights, roll_angles, atom_cot):
    highest = lax.Precision.HIGHEST
    slots = edge_feats.shape[0]
    experts, rows, _, width = weights.shape
    atoms_here = atom_cot.shape[0]
    group, crystals = lax.axis_size("mp"), lax.axis_size("dp")
    q = 2 * group * atoms_here
    scale = (atoms_here / slots) ** 0.5
    norm = (slots * group) ** (-0.5)
    crystal = lax.axis_index("dp")
    cot_rows = jnp.concatenate([atom_cot[:, :width], atom_cot[:, width:]], 0)
    cot_all = lax.all_gather(cot_rows, ("dp", "mp"), axis=0, tiled=True).reshape(crystals, q, width)
    cot = lax.dynamic_index_in_dim(cot_all, crystal, 0, False)

    coef_row = lax.dynamic_slice_in_dim(coefs, crystal, 1, 0)[0]
    flat = weights.reshape(experts, rows, 2, width // LANES, LANES).transpose(0, 1, 3, 2, 4)
    flat = flat.reshape(experts, rows * 2 * width // LANES, LANES)
    merged = jnp.sum(coef_row[:, None, None] * flat.astype(F32), 0).astype(BF16)
    merged = merged.reshape(rows, width // LANES, 2, LANES).transpose(2, 0, 1, 3).reshape(2 * rows, width)

    factor = scale * (jnp.arange(slots) < counts[0]).astype(F32)[:, None]
    cosine = (jnp.cos(roll_angles)[roll_ids])[:, None] * factor
    sine = (jnp.sin(roll_angles)[roll_ids])[:, None] * factor
    col = jnp.arange(q)[None, :]
    hit = targets[:, None] == col // 16 * 8 + col % 8
    real = col // 8 % 2 == 0
    spread_plus = jnp.where(hit, jnp.where(real, cosine, sine), 0.0).astype(BF16)
    spread_minus = jnp.where(hit, jnp.where(real, -sine, cosine), 0.0).astype(BF16)

    x_part = dot(edge_feats[:, :width], spread_plus, ((0,), (0,))) + dot(
        edge_feats[:, width:], spread_minus, ((0,), (0,))
    )
    x_here = lax.psum_scatter(x_part.astype(BF16), "mp", scatter_dimension=0, tiled=True)
    x_all = lax.all_gather(x_here[None], "dp", axis=0, tiled=True)
    x_wide = x_here.astype(F32)
    both = jnp.concatenate([x_wide, -turn(x_wide)], 0).astype(BF16)
    out_part = dot(both, merged, ((0,), (0,)))
    out = lax.psum_scatter(out_part.astype(BF16), "mp", scatter_dimension=0, tiled=True)
    atom_out = jnp.concatenate([out[:atoms_here], out[atoms_here:]], 1)

    back = dot(merged, cot, ((1,), (1,)))
    back = (back[:rows] + turn(back[rows:])).astype(BF16)
    back_all = lax.all_gather(back, "mp", axis=0, tiled=True)

    grad = dot(both, cot, ((1,), (0,))) * norm
    grad_flat = grad.reshape(2, rows, width // LANES, LANES).transpose(1, 2, 0, 3).reshape(-1, LANES)
    local_coef = jnp.sum(flat.astype(F32) * grad_flat[None], (1, 2))
    coef_grad = (lax.psum(local_coef, "mp") / width**0.5)[None, :]

    wg, edge_grad = mix(coefs, x_all, cot_all, back_all, jnp.stack([spread_plus, spread_minus]), norm)
    weight_grad = wg.reshape(experts, rows, width // LANES, 2, LANES).transpose(0, 1, 3, 2, 4)
    weight_grad = weight_grad.reshape(weights.shape)
    return (atom_out, edge_grad, weight_grad, coef_grad)


def solution(mesh):
    placed = (
        P(("dp", "mp"), None),
        P(("dp", "mp")),
        P(("dp", "mp")),
        P(("dp", "mp")),
        P(),
        P(None, "mp", None, None),
        P(),
        P(("dp", "mp"), None),
    )
    return jax.shard_map(
        on_device,
        mesh=mesh,
        in_specs=placed,
        out_specs=(
            P(("dp", "mp"), None),
            P(("dp", "mp"), None),
            P(None, "mp", None, None),
            P("dp", None),
        ),
        check_vma=False,
    )
```

```python
import functools

import jax
import jax.numpy as jnp
from jax import lax
from jax.experimental import pallas as pl
from jax.experimental.pallas import tpu as pltpu
from jax.sharding import PartitionSpec as P

BF16, F32 = jnp.bfloat16, jnp.float32
LANES = 128
MESH = pl.DeviceIdType.MESH
DP, MP = 8, 16
SLICES, COLS = 6, 256
ORDERS = (("z", "y", "x"), ("x", "z", "y"), ("y", "x", "z"))


def dot(a, b, contract):
    return lax.dot_general(a, b, (contract, ((), ())), preferred_element_type=F32)


def turn(rows):
    n = rows.shape[1]
    col = lax.broadcasted_iota(jnp.int32, rows.shape, 1)
    return jnp.where(col // 8 % 2 == 0, pltpu.roll(rows, n - 8, 1), -pltpu.roll(rows, 8, 1))


def interleave(wide, even, odd):
    n = even.shape[0]
    for h in range(2):
        wide[h, pl.ds(0, n, stride=2), :] = even[:, h * LANES : (h + 1) * LANES]
        wide[h, pl.ds(1, n, stride=2), :] = odd[:, h * LANES : (h + 1) * LANES]
    return jnp.concatenate([wide[0], wide[1]], 1)


def separate(wide, both):
    n = both.shape[0] // 2
    for h in range(2):
        wide[h] = both[:, h * LANES : (h + 1) * LANES]
    return [
        jnp.concatenate([wide[h, pl.ds(part, n, stride=2), :] for h in range(2)], 1) for part in range(2)
    ]


def remote(src, dst, send, recv, target):
    return pltpu.make_async_remote_copy(
        src_ref=src, dst_ref=dst, send_sem=send, recv_sem=recv, device_id=target, device_id_type=MESH
    )


def column_of(row):
    n = row.shape[1]
    same = lax.broadcasted_iota(jnp.int32, (n, n), 0) == lax.broadcasted_iota(jnp.int32, (n, n), 1)
    return jnp.sum(jnp.where(same, row, 0.0), 1, keepdims=True)


def exchange_kernel(
    scale, norm,
    feats_hbm, targets_ref, rolls_ref, counts_ref, coefs_ref, weights_hbm, angles_ref, cot_ref,
    atom_ref, coef_ref, spread_ref, x_hbm, back_hbm, cot_hbm,
    feats, weights, merged, mine, crystal, cots, x_parts, x_slots, x_all, back_all, out_parts, out_slots,
    coef_parts, wide,
    load_sem, weight_sem, store_sem,
    cry_s, cry_r, x_s, x_r, xd_s, xd_r, back_s, back_r, out_s, out_r, coef_s, coef_r,
    swap_s, swap_r, ring_s, ring_r, fin_s, fin_r,
):
    d, m = lax.axis_index("dp"), lax.axis_index("mp")
    z, y, x, core = d // 2, m // 8 * 2 + d % 2, m // 2 % 4, m % 2
    experts, rows = weights.shape[1], weights.shape[2]
    width = crystal.shape[2]
    tiles = width // LANES
    other = 1 - core
    sibling = (d, m + 1 - 2 * core)

    def device(z, y, x):
        return (z * 2 + y % 2, y // 2 * 8 + x * 2 + core)

    def mp_peer(j):
        return (d, lax.rem(m + j, MP))

    def dp_peer(j):
        return (lax.rem(d + j, DP), m)

    def each(n, body):
        lax.fori_loop(1, n, lambda j, c: (body(j), c)[1], 0)

    def span(start, stop, body):
        lax.fori_loop(start, stop, lambda j, c: (body(j), c)[1], 0)

    barrier = pltpu.get_barrier_semaphore()
    each(MP, lambda j: pl.semaphore_signal(barrier, inc=1, device_id=mp_peer(j), device_id_type=MESH))
    each(DP, lambda j: pl.semaphore_signal(barrier, inc=1, device_id=dp_peer(j), device_id_type=MESH))
    across = (d + 1 - 2 * (d % 2), lax.rem(m + 8, MP))
    pl.semaphore_signal(barrier, inc=1, device_id=across, device_id_type=MESH)

    feats_copy = pltpu.make_async_copy(feats_hbm, feats, load_sem)
    feats_copy.start()

    def weight_copy(t):
        return pltpu.make_async_copy(
            weights_hbm.at[:, :, :, pl.ds(pl.multiple_of(t * LANES, LANES), LANES)], weights.at[t], weight_sem.at[t]
        )

    span(0, tiles, lambda t: weight_copy(t).start())

    c = cot_ref[...].astype(F32)
    own = jnp.concatenate([c[:, :width], c[:, width:]], 0).astype(BF16)
    crystal[m] = own
    for s in range(SLICES):
        mine[s] = own[:, s * COLS : (s + 1) * COLS]
    for o in range(3):
        cots[3 * core + o, z, y, x, core] = mine[3 * core + o]

    slots = targets_ref.shape[1]
    table = rolls_ref[...] == lax.broadcasted_iota(jnp.int32, (angles_ref.shape[1], slots), 0)
    angle = column_of(angles_ref[...])
    valid = lax.broadcasted_iota(jnp.int32, (1, slots), 1) < counts_ref[0]
    factor = jnp.where(valid, scale, 0.0)
    cosine = column_of(jnp.sum(jnp.where(table, jnp.cos(angle), 0.0), 0, keepdims=True) * factor)
    sine = column_of(jnp.sum(jnp.where(table, jnp.sin(angle), 0.0), 0, keepdims=True) * factor)
    target = column_of(targets_ref[...].astype(F32)).astype(jnp.int32)
    q = lax.broadcasted_iota(jnp.int32, (slots, spread_ref.shape[2]), 1)
    hit = target == q // 16 * 8 + q % 8
    real = q // 8 % 2 == 0
    spread_ref[0] = jnp.where(hit, jnp.where(real, cosine, sine), 0.0).astype(BF16)
    spread_ref[1] = jnp.where(hit, jnp.where(real, -sine, cosine), 0.0).astype(BF16)

    pl.semaphore_wait(barrier, MP - 1 + DP - 1 + 1)

    swap = remote(
        mine.at[pl.ds(3 * other, 3)], cots.at[pl.ds(3 * other, 3), z, y, x, core], swap_s, swap_r, sibling
    )
    swap.start()
    each(MP, lambda j: remote(crystal.at[m], crystal.at[m], cry_s.at[j - 1], cry_r.at[j - 1], mp_peer(j)).start())

    here = {"z": z, "y": y, "x": x}

    def region(o, stage, value, half=None):
        order = ORDERS[o]
        index = dict(here)
        for a in order[:stage]:
            index[a] = slice(None)
        index[order[stage]] = value
        at = (3 * core + o, index["z"], index["y"], index["x"])
        return cots.at[at if half is None else at + (half,)]

    def neighbour(o, stage, by):
        to = dict(here)
        a = ORDERS[o][stage]
        to[a] = (here[a] + by) % 4
        return device(to["z"], to["y"], to["x"])

    def ring_copy(o, stage, kind):
        a = here[ORDERS[o][stage]]
        by = 1 if kind % 2 == 0 else 3
        value = a if kind < 2 else (a + 3) % 4 if kind == 2 else (a + 1) % 4
        ref = region(o, stage, value, None if kind < 2 else kind - 2)
        sem = (o * 3 + stage) * 4 + kind
        return remote(ref, ref, ring_s.at[sem], ring_r.at[sem], neighbour(o, stage, by))

    def ring_arrival(o, stage, kind):
        a = here[ORDERS[o][stage]]
        value = (a + 3) % 4 if kind == 0 else (a + 1) % 4 if kind == 1 else (a + 2) % 4
        ref = region(o, stage, value, None if kind < 2 else kind - 2)
        sem = (o * 3 + stage) * 4 + kind
        return remote(ref, ref, ring_s.at[sem], ring_r.at[sem], neighbour(o, stage, 1))

    def ring_first(stage):
        for o in range(3):
            for kind in (0, 1):
                ring_copy(o, stage, kind).start()

    def ring_second(stage):
        for o in range(3):
            for kind in (0, 1):
                ring_arrival(o, stage, kind).wait_recv()
                ring_copy(o, stage, kind + 2).start()

    def ring_end(stage):
        for o in range(3):
            for kind in (2, 3):
                ring_arrival(o, stage, kind).wait_recv()

    feats_copy.wait()
    group = 4
    block = group * rows

    def spread_block(i):
        plus = feats[:, pl.ds(pl.multiple_of(i * block, block), block)]
        minus = feats[:, pl.ds(pl.multiple_of(width + i * block, block), block)]
        part = dot(plus, spread_ref[0], ((0,), (0,))) + dot(minus, spread_ref[1], ((0,), (0,)))
        x_parts[pl.ds(i * group, group)] = part.astype(BF16).reshape(group, rows, -1)

    span(0, width // block, spread_block)

    def x_copy(j):
        return remote(
            x_parts.at[lax.rem(m + j, MP)], x_slots.at[j - 1], x_s.at[j - 1], x_r.at[j - 1], mp_peer(j)
        )

    each(MP, lambda j: x_copy(j).start())
    swap.wait_recv()
    ring_first(0)

    def merge(t):
        weight_copy(t).wait()
        total = jnp.zeros((2 * rows, LANES), F32)
        for k in range(experts):
            total += coefs_ref[d, k] * weights[t, k].reshape(2 * rows, LANES).astype(F32)
        merged[:, pl.ds(pl.multiple_of(t * LANES, LANES), LANES)] = total.astype(BF16)

    span(0, tiles // 3, merge)
    ring_second(0)
    span(tiles // 3, 2 * tiles // 3, merge)
    ring_end(0)
    ring_first(1)
    span(2 * tiles // 3, tiles, merge)

    def cry_copy(j):
        return remote(crystal.at[m], crystal.at[m], cry_s.at[j - 1], cry_r.at[j - 1], mp_peer(j))

    def cry_arrival(j):
        at = crystal.at[lax.rem(m - j + MP, MP)]
        return remote(at, at, cry_s.at[j - 1], cry_r.at[j - 1], mp_peer(j))

    each(MP, lambda j: cry_arrival(j).wait_recv())
    cot_rows = crystal[...].reshape(-1, width)
    by_real, by_imag = separate(wide, dot(merged[...], cot_rows, ((1,), (1,))))
    back_all[m] = (by_real + turn(by_imag)).astype(BF16)

    def back_copy(j):
        return remote(back_all.at[m], back_all.at[m], back_s.at[j - 1], back_r.at[j - 1], mp_peer(j))

    def back_arrival(j):
        at = back_all.at[lax.rem(m - j + MP, MP)]
        return remote(at, at, back_s.at[j - 1], back_r.at[j - 1], mp_peer(j))

    each(MP, lambda j: back_copy(j).start())
    ring_second(1)

    def x_add(j, total):
        x_copy(j).wait_recv()
        return total + x_slots[j - 1].astype(F32)

    x_here = lax.fori_loop(1, MP, x_add, x_parts[m].astype(F32)).astype(BF16)
    x_all[d] = x_here

    def xd_copy(j):
        return remote(x_all.at[d], x_all.at[d], xd_s.at[j - 1], xd_r.at[j - 1], dp_peer(j))

    def xd_arrival(j):
        at = x_all.at[lax.rem(d - j + DP, DP)]
        return remote(at, at, xd_s.at[j - 1], xd_r.at[j - 1], dp_peer(j))

    each(DP, lambda j: xd_copy(j).start())
    x_wide = x_here.astype(F32)
    both = interleave(wide, x_wide, -turn(x_wide)).astype(BF16)

    def out_block(i):
        cols = pl.ds(pl.multiple_of(i * block, block), block)
        sent = dot(both, merged[:, cols], ((0,), (0,))).astype(BF16)
        out_parts[:, :, cols] = sent.reshape(MP, 16, block)

    span(0, width // block, out_block)

    def out_copy(j):
        return remote(
            out_parts.at[lax.rem(m + j, MP)], out_slots.at[j - 1], out_s.at[j - 1], out_r.at[j - 1], mp_peer(j)
        )

    each(MP, lambda j: out_copy(j).start())
    ring_end(1)
    ring_first(2)

    def coef_add(t, sums):
        cols = pl.ds(pl.multiple_of(t * LANES, LANES), LANES)
        grad = dot(both, crystal[:, :, cols].reshape(-1, LANES), ((1,), (0,))) * norm
        added = []
        for k in range(experts):
            terms = weights[t, k].reshape(2 * rows, LANES).astype(F32) * grad
            added.append(sums[k] + jnp.sum(terms.reshape(-1, 8, LANES), 0))
        return tuple(added)

    sums = tuple(jnp.zeros((8, LANES), F32) for _ in range(experts))
    sums = lax.fori_loop(0, tiles // 2, coef_add, sums)
    ring_second(2)
    sums = lax.fori_loop(tiles // 2, tiles, coef_add, sums)
    coef_parts[0] = jnp.concatenate([jnp.sum(v, 0, keepdims=True) for v in sums], 0)

    def coef_copy(j):
        return remote(coef_parts.at[0], coef_parts.at[j], coef_s.at[j - 1], coef_r.at[j - 1], mp_peer(j))

    each(MP, lambda j: coef_copy(j).start())

    ring_end(2)

    def fin_copy(o):
        at = cots.at[3 * core + o]
        return remote(at, at, fin_s.at[o], fin_r.at[o], sibling)

    def fin_arrival(o):
        at = cots.at[3 * other + o]
        return remote(at, at, fin_s.at[o], fin_r.at[o], sibling)

    def cot_store(s, n):
        return pltpu.make_async_copy(cots.at[s], cot_hbm.at[s], store_sem.at[n])

    for o in range(3):
        fin_copy(o).start()
        cot_store(3 * core + o, o).start()

    each(MP, lambda j: back_arrival(j).wait_recv())
    back_store = pltpu.make_async_copy(back_all, back_hbm, store_sem.at[6])
    back_store.start()
    each(DP, lambda j: xd_arrival(j).wait_recv())
    x_store = pltpu.make_async_copy(x_all, x_hbm, store_sem.at[7])
    x_store.start()

    def out_add(j, out):
        out_copy(j).wait_recv()
        return out + out_slots[j - 1].astype(F32)

    out = lax.fori_loop(1, MP, out_add, out_parts[m].astype(F32))
    atom_ref[...] = jnp.concatenate([out[:8], out[8:]], 1).astype(BF16)

    each(MP, lambda j: coef_copy(j).wait_recv())
    lanes = jnp.sum(jnp.sum(coef_parts[...], 0), 1, keepdims=True) * (width**-0.5)
    same = lax.broadcasted_iota(jnp.int32, (experts, experts), 0) == lax.broadcasted_iota(
        jnp.int32, (experts, experts), 1
    )
    coef_ref[...] = jnp.sum(jnp.where(same, lanes, 0.0), 0, keepdims=True)

    for o in range(3):
        fin_arrival(o).wait_recv()
        cot_store(3 * other + o, 3 + o).start()

    swap.wait_send()
    each(MP, lambda j: cry_copy(j).wait_send())
    each(MP, lambda j: x_copy(j).wait_send())
    each(MP, lambda j: back_copy(j).wait_send())
    each(DP, lambda j: xd_copy(j).wait_send())
    each(MP, lambda j: out_copy(j).wait_send())
    each(MP, lambda j: coef_copy(j).wait_send())
    for o in range(3):
        for stage in range(3):
            for kind in range(4):
                ring_copy(o, stage, kind).wait_send()
        fin_copy(o).wait_send()
        cot_store(3 * core + o, o).wait()
        cot_store(3 * other + o, 3 + o).wait()
    back_store.wait()
    x_store.wait()


def exchange(edge_feats, targets, roll_ids, counts, coefs, weights, roll_angles, atom_cot):
    slots, double = edge_feats.shape
    width = double // 2
    experts, rows = weights.shape[:2]
    atoms_here = atom_cot.shape[0]
    q = 2 * MP * atoms_here
    vmem = pl.BlockSpec(memory_space=pltpu.VMEM)
    smem = pl.BlockSpec(memory_space=pltpu.SMEM)
    hbm = pl.BlockSpec(memory_space=pl.ANY)
    dma = pltpu.SemaphoreType.DMA
    cots = (SLICES, 4, 4, 4, 2, 16, COLS)
    return pl.pallas_call(
        functools.partial(
            exchange_kernel, (atoms_here / slots) ** 0.5, (slots * MP) ** -0.5
        ),
        in_specs=[hbm, vmem, vmem, smem, smem, hbm, vmem, vmem],
        out_specs=[vmem, vmem, vmem, hbm, hbm, hbm],
        out_shape=[
            jax.ShapeDtypeStruct(atom_cot.shape, BF16),
            jax.ShapeDtypeStruct((1, experts), F32),
            jax.ShapeDtypeStruct((2, slots, q), BF16),
            jax.ShapeDtypeStruct((DP, rows, q), BF16),
            jax.ShapeDtypeStruct((MP, rows, q), BF16),
            jax.ShapeDtypeStruct(cots, BF16),
        ],
        scratch_shapes=[
            pltpu.VMEM(edge_feats.shape, BF16),
            pltpu.VMEM((width // LANES, experts, rows, 2, LANES), BF16),
            pltpu.VMEM((2 * rows, width), BF16),
            pltpu.VMEM((SLICES, 16, COLS), BF16),
            pltpu.VMEM((MP, 16, width), BF16),
            pltpu.VMEM(cots, BF16),
            pltpu.VMEM((MP, rows, q), BF16),
            pltpu.VMEM((MP - 1, rows, q), BF16),
            pltpu.VMEM((DP, rows, q), BF16),
            pltpu.VMEM((MP, rows, q), BF16),
            pltpu.VMEM((MP, 16, width), BF16),
            pltpu.VMEM((MP - 1, 16, width), BF16),
            pltpu.VMEM((MP, experts, LANES), F32),
            pltpu.VMEM((2, 2 * rows, LANES), F32),
            dma(()), dma((width // LANES,)), dma((8,)),
        ]
        + [dma((n - 1,)) for n in (MP, MP, DP, MP, MP, MP) for _ in range(2)]
        + [dma(()), dma(()), dma((36,)), dma((36,)), dma((3,)), dma((3,))],
        compiler_params=pltpu.CompilerParams(
            collective_id=0, has_side_effects=True, vmem_limit_bytes=56 * 2**20
        ),
        cost_estimate=pl.CostEstimate(flops=4 * 10**9, bytes_accessed=2 * 10**7, transcendentals=0),
    )(
        edge_feats, targets[None], roll_ids[None], counts, coefs, weights, roll_angles[None], atom_cot
    )


def mix_kernel(norm, coefs_ref, x_ref, cot_ref, back_ref, spread_ref, wg_hbm, eg_ref, both_ref, wide, gm_ref, left_ref,
               out_ref, sem):
    step, steps = pl.program_id(0), pl.num_programs(0)
    crystals, rows, _ = x_ref.shape
    experts = wg_hbm.shape[0]

    @pl.when(step == 0)
    def _():
        r = lax.broadcasted_iota(jnp.int32, (16 * experts, 16 * crystals), 0)
        c = lax.broadcasted_iota(jnp.int32, (16 * experts, 16 * crystals), 1)
        pieces = []
        for k in range(experts):
            row = jnp.zeros((16, 16 * crystals), F32)
            for i in range(crystals):
                row = jnp.where(c[:16] // 16 == i, coefs_ref[i, k], row)
            pieces.append(row)
        mixed = jnp.where(r % 16 == c % 16, jnp.concatenate(pieces, 0), 0.0)
        high = mixed.astype(BF16)
        left_ref[:, : 16 * crystals] = high
        left_ref[:, 16 * crystals :] = (mixed - high.astype(F32)).astype(BF16)
        for i in range(crystals):
            x = x_ref[i].astype(F32)
            both_ref[i] = interleave(wide, x, -turn(x)).astype(BF16)

    for i in range(crystals):
        cot = jnp.concatenate(
            [cot_ref[0, i // 2, i % 2 + 2 * h].reshape(LANES, COLS) for h in range(2)], 0
        )
        gm_ref[i] = (dot(both_ref[i], cot, ((1,), (0,))) * norm).astype(BF16)

    slot = lax.rem(step, 2)

    def copies(step):
        slot = lax.rem(step, 2)
        return [
            pltpu.make_async_copy(
                out_ref.at[slot, t],
                wg_hbm.at[:, :, :, pl.ds(pl.multiple_of(step * COLS + t * LANES, LANES), LANES)],
                sem.at[slot, t],
            )
            for t in range(2)
        ]

    @pl.when(step >= 2)
    def _():
        for copy in copies(step - 2):
            copy.wait()

    for g in range(2 * rows // 16):
        right = jnp.concatenate([gm_ref[i, g * 16 : (g + 1) * 16, :] for i in range(crystals)] * 2, 0)
        out = dot(left_ref[...], right, ((1,), (0,))).astype(BF16)
        for t in range(2):
            for k in range(experts):
                piece = out[k * 16 : (k + 1) * 16, t * LANES : (t + 1) * LANES]
                out_ref[slot, t, k, g * 8 : (g + 1) * 8] = piece.reshape(8, 2, LANES)

    for copy in copies(step):
        copy.start()

    part = step // (steps // 2)
    cols = eg_ref.shape[1]
    at = pl.multiple_of(step % (steps // 2) * cols, cols)
    eg_ref[...] = dot(spread_ref[part], back_ref[pl.ds(at, cols), :], ((1,), (1,))).astype(BF16)

    @pl.when(step == steps - 1)
    def _():
        for copy in copies(step - 1) + copies(step):
            copy.wait()


def mix(coefs, x_all, cot_all, back_all, spread, norm):
    crystals, experts = coefs.shape
    _, rows, q = x_all.shape
    width = back_all.shape[0]
    slots = spread.shape[1]
    whole = lambda shape: pl.BlockSpec(shape, lambda i: (0,) * len(shape))
    return pl.pallas_call(
        functools.partial(mix_kernel, norm),
        grid=(SLICES,),
        in_specs=[
            pl.BlockSpec(memory_space=pltpu.SMEM),
            whole(x_all.shape),
            pl.BlockSpec((1,) + cot_all.shape[1:], lambda i: (i,) + (0,) * 6),
            whole(back_all.shape),
            whole(spread.shape),
        ],
        out_specs=[
            pl.BlockSpec(memory_space=pl.ANY),
            pl.BlockSpec((slots, 2 * width // SLICES), lambda i: (0, i)),
        ],
        out_shape=[
            jax.ShapeDtypeStruct((experts, rows, 2, width), BF16),
            jax.ShapeDtypeStruct((slots, 2 * width), BF16),
        ],
        scratch_shapes=[
            pltpu.VMEM((crystals, 2 * rows, q), BF16),
            pltpu.VMEM((2, 2 * rows, LANES), F32),
            pltpu.VMEM((crystals, 2 * rows, COLS), BF16),
            pltpu.VMEM((16 * experts, 32 * crystals), BF16),
            pltpu.VMEM((2, 2, experts, rows, 2, LANES), BF16),
            pltpu.SemaphoreType.DMA((2, 2)),
        ],
        compiler_params=pltpu.CompilerParams(vmem_limit_bytes=40 * 2**20),
        cost_estimate=pl.CostEstimate(flops=10**10, bytes_accessed=2 * 10**7, transcendentals=0),
    )(coefs, x_all, cot_all, back_all, spread)


def on_device(edge_feats, targets, roll_ids, counts, coefs, weights, roll_angles, atom_cot):
    slots = edge_feats.shape[0]
    atom_out, coef_grad, spread, x_all, back_all, cot_all = exchange(
        edge_feats, targets, roll_ids, counts, coefs, weights, roll_angles, atom_cot
    )
    back_all = back_all.reshape(-1, back_all.shape[2])
    weight_grad, edge_grad = mix(coefs, x_all, cot_all, back_all, spread, (slots * MP) ** -0.5)
    return (atom_out, edge_grad, weight_grad, coef_grad)


def solution(mesh):
    placed = (
        P(("dp", "mp"), None),
        P(("dp", "mp")),
        P(("dp", "mp")),
        P(("dp", "mp")),
        P(),
        P(None, "mp", None, None),
        P(),
        P(("dp", "mp"), None),
    )
    return jax.shard_map(
        on_device,
        mesh=mesh,
        in_specs=placed,
        out_specs=(
            P(("dp", "mp"), None),
            P(("dp", "mp"), None),
            P(None, "mp", None, None),
            P("dp", None),
        ),
        check_vma=False,
    )
```

```python
import functools

import jax
import jax.numpy as jnp
from jax import lax
from jax.experimental import pallas as pl
from jax.experimental.pallas import tpu as pltpu
from jax.sharding import PartitionSpec as P

BF16, F32 = jnp.bfloat16, jnp.float32
LANES = 128
MESH = pl.DeviceIdType.MESH
DP, MP = 8, 16
SLICES, COLS = 6, 256
ORDERS = (("x", "y", "z"), ("y", "x", "z"), ("z", "x", "y"))
SWAP, RING, PLANE, X_SUM, OUT_SUM, BACK, X_DP, COEF = 0, 1, 37, 49, 55, 61, 70, 75
COPIES = COEF + MP - 1


def dot(a, b, contract):
    return lax.dot_general(a, b, (contract, ((), ())), preferred_element_type=F32)


def turn(rows):
    n = rows.shape[1]
    col = lax.broadcasted_iota(jnp.int32, rows.shape, 1)
    return jnp.where(col // 8 % 2 == 0, pltpu.roll(rows, n - 8, 1), -pltpu.roll(rows, 8, 1))


def interleave(wide, even, odd):
    n = even.shape[0]
    for h in range(2):
        wide[h, pl.ds(0, n, stride=2), :] = even[:, h * LANES : (h + 1) * LANES]
        wide[h, pl.ds(1, n, stride=2), :] = odd[:, h * LANES : (h + 1) * LANES]
    return jnp.concatenate([wide[0], wide[1]], 1)


def separate(wide, both):
    n = both.shape[0] // 2
    for h in range(2):
        wide[h] = both[:, h * LANES : (h + 1) * LANES]
    return [
        jnp.concatenate([wide[h, pl.ds(part, n, stride=2), :] for h in range(2)], 1) for part in range(2)
    ]


def remote(src, dst, send, recv, target):
    return pltpu.make_async_remote_copy(
        src_ref=src, dst_ref=dst, send_sem=send, recv_sem=recv, device_id=target, device_id_type=MESH
    )


def column_of(row):
    n = row.shape[1]
    same = lax.broadcasted_iota(jnp.int32, (n, n), 0) == lax.broadcasted_iota(jnp.int32, (n, n), 1)
    return jnp.sum(jnp.where(same, row, 0.0), 1, keepdims=True)


def exchange_kernel(
    scale, norm,
    feats_hbm, targets_ref, rolls_ref, counts_ref, coefs_ref, weights_hbm, angles_ref, cot_ref,
    atom_ref, coef_ref, spread_ref, x_hbm, back_hbm, cot_hbm,
    feats, weights, merged, mine, crystal, cots, x_all, back_all, coef_parts, wide,
    x_parts, x_pair, x_held, x_one, x_two, x_cross, out_parts, out_pair, out_held, out_one, out_two, out_cross,
    load_sem, weight_sem, store_sem, send_sem, recv_sem,
):
    d, m = lax.axis_index("dp"), lax.axis_index("mp")
    z, y, x, core = d // 2, m // 8 * 2 + d % 2, m // 2 % 4, m % 2
    y_hi, y_lo = m // 8, d % 2
    tiles, experts, double, _ = weights.shape
    rows, width = double // 2, tiles * LANES
    other = 1 - core
    ahead, behind, far = (x + 1) % 4, (x + 3) % 4, (x + 2) % 4

    def device(z, y, x, core):
        return (z * 2 + y % 2, y // 2 * 8 + x * 2 + core)

    sibling = device(z, y, x, other)
    x_next, x_last = device(z, y, ahead, core), device(z, y, behind, core)
    y_peer = device(z, (y + 2) % 4, x, core)
    z_next, z_last = device((z + 1) % 4, y, x, core), device((z + 3) % 4, y, x, core)
    y_next, y_last = device(z, (y + 1) % 4, x, core), device(z, (y + 3) % 4, x, core)
    lo_peer = (d + 1 - 2 * y_lo, m)

    def mp_peer(j):
        return (d, lax.rem(m + j, MP))

    def span(start, stop, body):
        lax.fori_loop(start, stop, lambda j, c: (body(j), c)[1], 0)

    barrier = pltpu.get_barrier_semaphore()
    span(1, MP, lambda j: pl.semaphore_signal(barrier, inc=1, device_id=mp_peer(j), device_id_type=MESH))
    for to in (z_next, z_last, y_next, y_last):
        pl.semaphore_signal(barrier, inc=1, device_id=to, device_id_type=MESH)

    feats_copy = pltpu.make_async_copy(feats_hbm, feats, load_sem)
    feats_copy.start()
    weight_rows = weights_hbm.reshape(experts, double, width)

    def weight_copy(t):
        cols = pl.ds(pl.multiple_of(t * LANES, LANES), LANES)
        return pltpu.make_async_copy(weight_rows.at[:, :, cols], weights.at[t], weight_sem.at[t])

    span(0, tiles, lambda t: weight_copy(t).start())

    sent = []

    def send(sem, src, dst, to):
        copy = remote(src, dst, send_sem.at[sem], recv_sem.at[sem], to)
        copy.start()
        sent.append(copy)

    def arrive(sem, ref):
        remote(ref, ref, send_sem.at[sem], recv_sem.at[sem], sibling).wait_recv()

    c = cot_ref[...].astype(F32)
    own = jnp.concatenate([c[:, :width], c[:, width:]], 0).astype(BF16)
    for s in range(SLICES):
        mine[s] = own[:, s * COLS : (s + 1) * COLS]
    for o in range(3):
        cots[3 * core + o, z, y, x, core] = mine[3 * core + o]

    slots = targets_ref.shape[1]
    table = rolls_ref[...] == lax.broadcasted_iota(jnp.int32, (angles_ref.shape[1], slots), 0)
    angle = column_of(angles_ref[...])
    valid = lax.broadcasted_iota(jnp.int32, (1, slots), 1) < counts_ref[0]
    factor = jnp.where(valid, scale, 0.0)
    cosine = column_of(jnp.sum(jnp.where(table, jnp.cos(angle), 0.0), 0, keepdims=True) * factor)
    sine = column_of(jnp.sum(jnp.where(table, jnp.sin(angle), 0.0), 0, keepdims=True) * factor)
    target = column_of(targets_ref[...].astype(F32)).astype(jnp.int32)
    q = lax.broadcasted_iota(jnp.int32, (slots, spread_ref.shape[2]), 1)
    hit = target == q // 16 * 8 + q % 8
    real = q // 8 % 2 == 0
    spread_ref[0] = jnp.where(hit, jnp.where(real, cosine, sine), 0.0).astype(BF16)
    spread_ref[1] = jnp.where(hit, jnp.where(real, -sine, cosine), 0.0).astype(BF16)

    pl.semaphore_wait(barrier, MP - 1 + 4)

    theirs = pl.ds(3 * other, 3)
    send(SWAP, mine.at[theirs], cots.at[theirs, z, y, x, core], sibling)

    here = {"z": z, "y": y, "x": x}
    nexts = {"z": (z_next, z_last), "y": (y_next, y_last), "x": (x_next, x_last)}

    def region(o, stage, value, half=None):
        order = ORDERS[o]
        index = dict(here)
        for a in order[:stage]:
            index[a] = slice(None)
        index[order[stage]] = value
        at = (3 * core + o, index["z"], index["y"], index["x"])
        return cots.at[at if half is None else at + (half,)]

    def ring_send(o, stage, kind):
        axis = ORDERS[o][stage]
        a = here[axis]
        value = (a, a, (a + 3) % 4, (a + 1) % 4)[kind]
        ref = region(o, stage, value, None if kind < 2 else kind - 2)
        send(RING + (o * 3 + stage) * 4 + kind, ref, ref, nexts[axis][kind % 2])

    def ring_arrive(o, stage, kind):
        a = here[ORDERS[o][stage]]
        value = ((a + 3) % 4, (a + 1) % 4, (a + 2) % 4, (a + 2) % 4)[kind]
        arrive(RING + (o * 3 + stage) * 4 + kind, region(o, stage, value, None if kind < 2 else kind - 2))

    def ring_first(stage, which=(0, 1, 2)):
        for o in which:
            for kind in (0, 1):
                ring_send(o, stage, kind)

    def ring_second(stage, which=(0, 1, 2)):
        for o in which:
            for kind in (0, 1):
                ring_arrive(o, stage, kind)
                ring_send(o, stage, kind + 2)

    def ring_end(stage, which=(0, 1, 2)):
        for o in which:
            for kind in (2, 3):
                ring_arrive(o, stage, kind)

    def plane_send(o, by):
        ref = cots.at[3 * core + o, (z + by) % 4]
        send(PLANE + o * 4 + by, ref, ref, sibling)

    def plane_arrive(o, by):
        arrive(PLANE + o * 4 + by, cots.at[3 * other + o, (z + by) % 4])

    def sum_cores(base, parts, pair):
        send(base, parts.at[other], pair, sibling)

    def sum_x(base, parts, pair, held, one):
        arrive(base, pair)
        for h in range(2):
            for i in range(4):
                held[i, h] = (parts[core, h, i].astype(F32) + pair[h, i].astype(F32)).astype(BF16)
        send(base + 1, held.at[far, 0], one.at[0], x_next)
        send(base + 2, held.at[far, 1], one.at[1], x_last)

    def sum_x_more(base, held, one, two):
        for h, to, at in ((0, x_next, ahead), (1, x_last, behind)):
            arrive(base + 1 + h, one.at[h])
            held[at, h] = (held[at, h].astype(F32) + one[h].astype(F32)).astype(BF16)
            send(base + 3 + h, held.at[at], two.at[h], to)

    def sum_of(held, two, h):
        return held[x, h].astype(F32) + two[0, h].astype(F32) + two[1, h].astype(F32)

    def sum_y(base, held, two, cross):
        for h in range(2):
            arrive(base + 3 + h, two.at[h])
        cross[0] = sum_of(held, two, 1 - y_hi).astype(BF16)
        send(base + 5, cross.at[0], cross.at[1], y_peer)

    def sum_end(base, held, two, cross):
        arrive(base + 5, cross.at[1])
        return sum_of(held, two, y_hi) + cross[1].astype(F32)

    feats_copy.wait()
    group = 4
    block = group * rows

    def spread_block(i):
        plus = feats[:, pl.ds(pl.multiple_of(i * block, block), block)]
        minus = feats[:, pl.ds(pl.multiple_of(width + i * block, block), block)]
        part = dot(plus, spread_ref[0], ((0,), (0,))) + dot(minus, spread_ref[1], ((0,), (0,)))
        part = part.astype(BF16)
        for g in range(group):
            x_parts[g % 2, i // 2, i % 2 * 2 + g // 2] = part[g * rows : (g + 1) * rows]

    span(0, width // block, spread_block)
    sum_cores(X_SUM, x_parts, x_pair)
    arrive(SWAP, cots.at[pl.ds(3 * core, 3), z, y, x, other])
    ring_first(0)

    def merge(t):
        weight_copy(t).wait()
        total = jnp.zeros((double, LANES), F32)
        for k in range(experts):
            total += coefs_ref[d, k] * weights[t, k].astype(F32)
        merged[:, pl.ds(pl.multiple_of(t * LANES, LANES), LANES)] = total.astype(BF16)

    span(0, tiles // 4, merge)
    sum_x(X_SUM, x_parts, x_pair, x_held, x_one)
    ring_second(0)
    span(tiles // 4, tiles // 2, merge)
    sum_x_more(X_SUM, x_held, x_one, x_two)
    ring_end(0)
    ring_first(1)
    span(tiles // 2, 3 * tiles // 4, merge)
    sum_y(X_SUM, x_held, x_two, x_cross)
    ring_second(1)
    span(3 * tiles // 4, tiles, merge)
    ring_end(1, (2,))
    ring_first(2, (2,))
    ring_end(1, (0, 1))
    ring_first(2, (0, 1))
    for o in range(2):
        plane_send(o, 0)

    x_here = sum_end(X_SUM, x_held, x_two, x_cross).astype(BF16)
    x_all[d] = x_here
    send(X_DP, x_all.at[d], x_all.at[d], lo_peer)
    x_wide = x_here.astype(F32)
    both = interleave(wide, x_wide, -turn(x_wide))
    both_turned = both.T.astype(BF16)
    both = both.astype(BF16)

    def out_block(i):
        cols = pl.ds(pl.multiple_of(i * block, block), block)
        part = dot(both_turned, merged[:, cols], ((1,), (0,))).astype(BF16)
        for p in range(MP):
            out_parts[p % 2, p // 8, p // 2 % 4, :, cols] = part[p * 16 : (p + 1) * 16]

    span(0, width // block, out_block)
    sum_cores(OUT_SUM, out_parts, out_pair)

    pair = x_all.at[pl.ds(2 * z, 2)]
    arrive(X_DP, x_all.at[d + 1 - 2 * y_lo])
    send(X_DP + 1, pair, pair, z_next)
    send(X_DP + 2, pair, pair, z_last)

    sum_x(OUT_SUM, out_parts, out_pair, out_held, out_one)
    ring_second(2, (2,))
    sum_x_more(OUT_SUM, out_held, out_one, out_two)

    for h, to, by in ((0, z_next, 3), (1, z_last, 1)):
        arrive(X_DP + 1 + h, x_all.at[pl.ds((z + by) % 4 * 2, 2)])
        ref = x_all.at[(z + by) % 4 * 2 + h]
        send(X_DP + 3 + h, ref, ref, to)

    ring_end(2, (2,))
    for by in range(4):
        plane_send(2, by)
    sum_y(OUT_SUM, out_held, out_two, out_cross)

    for o in range(3):
        plane_arrive(o, 0)
    for s in range(SLICES):
        for h in range(2):
            crystal[h * LANES : (h + 1) * LANES, s * COLS : (s + 1) * COLS] = cots[s, z, y_lo + 2 * h].reshape(
                LANES, COLS
            )
    by_real, by_imag = separate(wide, dot(merged[...], crystal[...], ((1,), (1,))))
    back_all[y_hi, x, core] = (by_real + turn(by_imag)).astype(BF16)
    low = 1 - y_hi
    mine_back = back_all.at[y_hi, x, core]
    send(BACK, mine_back, mine_back, y_peer)
    send(BACK + 1, mine_back, mine_back, x_next)
    send(BACK + 2, mine_back, mine_back, x_last)
    ring_second(2, (0, 1))
    peer_back = back_all.at[low, x, core]
    arrive(BACK, peer_back)
    send(BACK + 3, peer_back, peer_back, x_next)
    send(BACK + 4, peer_back, peer_back, x_last)

    def coef_add(t, sums):
        cols = pl.ds(pl.multiple_of(t * LANES, LANES), LANES)
        grad = dot(both, crystal[:, cols], ((1,), (0,))) * norm
        added = []
        for k in range(experts):
            terms = weights[t, k].astype(F32) * grad
            added.append(sums[k] + jnp.sum(terms.reshape(-1, 8, LANES), 0))
        return tuple(added)

    sums = tuple(jnp.zeros((8, LANES), F32) for _ in range(experts))
    sums = lax.fori_loop(0, tiles // 2, coef_add, sums)
    arrive(BACK + 1, back_all.at[y_hi, behind, core])
    send(BACK + 5, back_all.at[y_hi, behind, core], back_all.at[y_hi, behind, core], x_next)
    arrive(BACK + 4, back_all.at[low, ahead, core])
    send(BACK + 6, back_all.at[low, ahead, core], back_all.at[low, ahead, core], x_last)
    sums = lax.fori_loop(tiles // 2, tiles, coef_add, sums)
    lanes = jnp.sum(jnp.concatenate([jnp.sum(v, 0, keepdims=True) for v in sums], 0), 1, keepdims=True)
    same = lax.broadcasted_iota(jnp.int32, (experts, LANES), 0) == lax.broadcasted_iota(
        jnp.int32, (experts, LANES), 1
    )
    coef_parts[0] = jnp.sum(jnp.where(same, lanes, 0.0), 0, keepdims=True)

    def coef_copy(j):
        sem = COEF + j - 1
        return remote(coef_parts.at[0], coef_parts.at[j], send_sem.at[sem], recv_sem.at[sem], mp_peer(j))

    span(1, MP, lambda j: coef_copy(j).start())

    out = sum_end(OUT_SUM, out_held, out_two, out_cross)
    half = out.shape[0] // 2
    atom_ref[...] = jnp.concatenate([out[:half], out[half:]], 1).astype(BF16)

    arrive(BACK + 2, back_all.at[y_hi, ahead, core])
    arrive(BACK + 3, back_all.at[low, behind, core])
    arrive(BACK + 5, back_all.at[y_hi, far, core])
    arrive(BACK + 6, back_all.at[low, far, core])
    send(BACK + 7, back_all.at[0, :, core], back_all.at[0, :, core], sibling)
    send(BACK + 8, back_all.at[1, :, core], back_all.at[1, :, core], sibling)

    ring_end(2, (0, 1))
    for by in range(1, 4):
        for o in range(2):
            plane_send(o, by)

    stores = []

    def store(src, dst):
        copy = pltpu.make_async_copy(src, dst, store_sem.at[len(stores)])
        copy.start()
        stores.append(copy)

    for o in range(3):
        store(cots.at[3 * core + o], cot_hbm.at[3 * core + o])
    for h, by in ((0, 3), (1, 1)):
        arrive(X_DP + 3 + h, x_all.at[(z + 2) % 4 * 2 + h])
    store(x_all, x_hbm)
    arrive(BACK + 7, back_all.at[0, :, other])
    arrive(BACK + 8, back_all.at[1, :, other])
    store(back_all, back_hbm)

    span(1, MP, lambda j: coef_copy(j).wait_recv())
    coef_ref[...] = jnp.sum(coef_parts[...], 0)[:, :experts] * (width**-0.5)

    for by in range(4):
        for o in range(3):
            if by > 0:
                plane_arrive(o, by)
            at = (3 * other + o, (z + by) % 4)
            store(cots.at[at], cot_hbm.at[at])

    span(1, MP, lambda j: coef_copy(j).wait_send())
    for copy in sent:
        copy.wait_send()
    for copy in stores:
        copy.wait()


def exchange(edge_feats, targets, roll_ids, counts, coefs, weights, roll_angles, atom_cot):
    slots, wide = edge_feats.shape
    width = wide // 2
    experts, rows = weights.shape[:2]
    atoms_here = atom_cot.shape[0]
    q = 2 * MP * atoms_here
    vmem = pl.BlockSpec(memory_space=pltpu.VMEM)
    smem = pl.BlockSpec(memory_space=pltpu.SMEM)
    hbm = pl.BlockSpec(memory_space=pl.ANY)
    dma = pltpu.SemaphoreType.DMA
    cots = (SLICES, 4, 4, 4, 2, 16, COLS)
    sums = [
        pltpu.VMEM(lead + block, BF16)
        for block in ((rows, q), (16, width))
        for lead in ((2, 2, 4), (2, 4), (4, 2), (2,), (2, 2), (2,))
    ]
    return pl.pallas_call(
        functools.partial(exchange_kernel, (atoms_here / slots) ** 0.5, (slots * MP) ** -0.5),
        in_specs=[hbm, vmem, vmem, smem, smem, hbm, vmem, vmem],
        out_specs=[vmem, vmem, vmem, hbm, hbm, hbm],
        out_shape=[
            jax.ShapeDtypeStruct(atom_cot.shape, BF16),
            jax.ShapeDtypeStruct((1, experts), F32),
            jax.ShapeDtypeStruct((2, slots, q), BF16),
            jax.ShapeDtypeStruct((DP, rows, q), BF16),
            jax.ShapeDtypeStruct((2, 4, 2, rows, q), BF16),
            jax.ShapeDtypeStruct(cots, BF16),
        ],
        scratch_shapes=[
            pltpu.VMEM(edge_feats.shape, BF16),
            pltpu.VMEM((width // LANES, experts, 2 * rows, LANES), BF16),
            pltpu.VMEM((2 * rows, width), BF16),
            pltpu.VMEM((SLICES, 16, COLS), BF16),
            pltpu.VMEM((q, width), BF16),
            pltpu.VMEM(cots, BF16),
            pltpu.VMEM((DP, rows, q), BF16),
            pltpu.VMEM((2, 4, 2, rows, q), BF16),
            pltpu.VMEM((MP, 1, LANES), F32),
            pltpu.VMEM((2, 2 * rows, LANES), F32),
            *sums,
            dma(()), dma((width // LANES,)), dma((17,)), dma((COPIES,)), dma((COPIES,)),
        ],
        compiler_params=pltpu.CompilerParams(
            collective_id=0, has_side_effects=True, vmem_limit_bytes=56 * 2**20
        ),
        cost_estimate=pl.CostEstimate(flops=4 * 10**9, bytes_accessed=2 * 10**7, transcendentals=0),
    )(
        edge_feats, targets[None], roll_ids[None], counts, coefs, weights, roll_angles[None], atom_cot
    )


def mix_kernel(norm, coefs_ref, x_ref, cot_ref, back_ref, spread_ref, wg_hbm, eg_ref, both_ref, wide, gm_ref, left_ref,
               out_ref, sem):
    step, steps = pl.program_id(0), pl.num_programs(0)
    crystals, rows, _ = x_ref.shape
    experts, _, _, width = wg_hbm.shape
    wg_rows = wg_hbm.reshape(experts, 2 * rows, width)

    @pl.when(step == 0)
    def _():
        r = lax.broadcasted_iota(jnp.int32, (16 * experts, 16 * crystals), 0)
        c = lax.broadcasted_iota(jnp.int32, (16 * experts, 16 * crystals), 1)
        pieces = []
        for k in range(experts):
            row = jnp.zeros((16, 16 * crystals), F32)
            for i in range(crystals):
                row = jnp.where(c[:16] // 16 == i, coefs_ref[i, k], row)
            pieces.append(row)
        mixed = jnp.where(r % 16 == c % 16, jnp.concatenate(pieces, 0), 0.0)
        high = mixed.astype(BF16)
        left_ref[:, : 16 * crystals] = high
        left_ref[:, 16 * crystals :] = (mixed - high.astype(F32)).astype(BF16)
        for i in range(crystals):
            x = x_ref[i].astype(F32)
            both_ref[i] = interleave(wide, x, -turn(x)).astype(BF16)

    for i in range(crystals):
        cot = jnp.concatenate(
            [cot_ref[0, i // 2, i % 2 + 2 * h].reshape(LANES, COLS) for h in range(2)], 0
        )
        gm_ref[i] = (dot(both_ref[i], cot, ((1,), (0,))) * norm).astype(BF16)

    slot = lax.rem(step, 2)

    def copies(step):
        slot = lax.rem(step, 2)
        return [
            pltpu.make_async_copy(
                out_ref.at[slot, t],
                wg_rows.at[:, :, pl.ds(pl.multiple_of(step * COLS + t * LANES, LANES), LANES)],
                sem.at[slot, t],
            )
            for t in range(2)
        ]

    @pl.when(step >= 2)
    def _():
        for copy in copies(step - 2):
            copy.wait()

    for g in range(2 * rows // 16):
        right = jnp.concatenate([gm_ref[i, g * 16 : (g + 1) * 16, :] for i in range(crystals)] * 2, 0)
        out = dot(left_ref[...], right, ((1,), (0,))).astype(BF16)
        for t in range(2):
            for k in range(experts):
                piece = out[k * 16 : (k + 1) * 16, t * LANES : (t + 1) * LANES]
                out_ref[slot, t, k, g * 16 : (g + 1) * 16] = piece

    for copy in copies(step):
        copy.start()

    part = step // (steps // 2)
    cols = eg_ref.shape[1]
    at = pl.multiple_of(step % (steps // 2) * cols, cols)
    eg_ref[...] = dot(spread_ref[part], back_ref[pl.ds(at, cols), :], ((1,), (1,))).astype(BF16)

    @pl.when(step == steps - 1)
    def _():
        for copy in copies(step - 1) + copies(step):
            copy.wait()


def mix(coefs, x_all, cot_all, back_all, spread, norm):
    crystals, experts = coefs.shape
    _, rows, q = x_all.shape
    width = back_all.shape[0]
    slots = spread.shape[1]
    whole = lambda shape: pl.BlockSpec(shape, lambda i: (0,) * len(shape))
    return pl.pallas_call(
        functools.partial(mix_kernel, norm),
        grid=(SLICES,),
        in_specs=[
            pl.BlockSpec(memory_space=pltpu.SMEM),
            whole(x_all.shape),
            pl.BlockSpec((1,) + cot_all.shape[1:], lambda i: (i,) + (0,) * 6),
            whole(back_all.shape),
            whole(spread.shape),
        ],
        out_specs=[
            pl.BlockSpec(memory_space=pl.ANY),
            pl.BlockSpec((slots, 2 * width // SLICES), lambda i: (0, i)),
        ],
        out_shape=[
            jax.ShapeDtypeStruct((experts, rows, 2, width), BF16),
            jax.ShapeDtypeStruct((slots, 2 * width), BF16),
        ],
        scratch_shapes=[
            pltpu.VMEM((crystals, 2 * rows, q), BF16),
            pltpu.VMEM((2, 2 * rows, LANES), F32),
            pltpu.VMEM((crystals, 2 * rows, COLS), BF16),
            pltpu.VMEM((16 * experts, 32 * crystals), BF16),
            pltpu.VMEM((2, 2, experts, 2 * rows, LANES), BF16),
            pltpu.SemaphoreType.DMA((2, 2)),
        ],
        compiler_params=pltpu.CompilerParams(vmem_limit_bytes=60 * 2**20),
        cost_estimate=pl.CostEstimate(flops=10**10, bytes_accessed=2 * 10**7, transcendentals=0),
    )(coefs, x_all, cot_all, back_all, spread)


def on_device(edge_feats, targets, roll_ids, counts, coefs, weights, roll_angles, atom_cot):
    slots = edge_feats.shape[0]
    atom_out, coef_grad, spread, x_all, back_all, cot_all = exchange(
        edge_feats, targets, roll_ids, counts, coefs, weights, roll_angles, atom_cot
    )
    back_all = back_all.reshape(-1, back_all.shape[-1])
    weight_grad, edge_grad = mix(coefs, x_all, cot_all, back_all, spread, (slots * MP) ** -0.5)
    return (atom_out, edge_grad, weight_grad, coef_grad)


def solution(mesh):
    placed = (
        P(("dp", "mp"), None),
        P(("dp", "mp")),
        P(("dp", "mp")),
        P(("dp", "mp")),
        P(),
        P(None, "mp", None, None),
        P(),
        P(("dp", "mp"), None),
    )
    return jax.shard_map(
        on_device,
        mesh=mesh,
        in_specs=placed,
        out_specs=(
            P(("dp", "mp"), None),
            P(("dp", "mp"), None),
            P(None, "mp", None, None),
            P("dp", None),
        ),
        check_vma=False,
    )
```

```python
import functools

import jax
import jax.numpy as jnp
from jax import lax
from jax.experimental import pallas as pl
from jax.experimental.pallas import tpu as pltpu
from jax.sharding import PartitionSpec as P

BF16, F32 = jnp.bfloat16, jnp.float32
LANES = 128
MESH = pl.DeviceIdType.MESH
DP, MP = 8, 16
SLICES, COLS = 6, 256
ORDERS = (("x", "y", "z"), ("z", "x", "y"), ("y", "z", "x"))
SWAP, RING, PLANE, X_SUM, OUT_SUM, COT, BACK, X_DP, COEF = 0, 1, 28, 40, 48, 56, 64, 72, 76
COPIES = COEF + MP - 1


def dot(a, b, contract):
    return lax.dot_general(a, b, (contract, ((), ())), preferred_element_type=F32)


def turn(rows):
    n = rows.shape[1]
    col = lax.broadcasted_iota(jnp.int32, rows.shape, 1)
    return jnp.where(col // 8 % 2 == 0, pltpu.roll(rows, n - 8, 1), -pltpu.roll(rows, 8, 1))


def interleave(wide, even, odd):
    n = even.shape[0]
    for h in range(2):
        wide[h, pl.ds(0, n, stride=2), :] = even[:, h * LANES : (h + 1) * LANES]
        wide[h, pl.ds(1, n, stride=2), :] = odd[:, h * LANES : (h + 1) * LANES]
    return jnp.concatenate([wide[0], wide[1]], 1)


def separate(wide, both):
    n = both.shape[0] // 2
    for h in range(2):
        wide[h] = both[:, h * LANES : (h + 1) * LANES]
    return [
        jnp.concatenate([wide[h, pl.ds(part, n, stride=2), :] for h in range(2)], 1) for part in range(2)
    ]


def remote(src, dst, send, recv, target):
    return pltpu.make_async_remote_copy(
        src_ref=src, dst_ref=dst, send_sem=send, recv_sem=recv, device_id=target, device_id_type=MESH
    )


def column_of(row):
    n = row.shape[1]
    same = lax.broadcasted_iota(jnp.int32, (n, n), 0) == lax.broadcasted_iota(jnp.int32, (n, n), 1)
    return jnp.sum(jnp.where(same, row, 0.0), 1, keepdims=True)


def exchange_kernel(
    scale, norm,
    feats_hbm, targets_ref, rolls_ref, counts_ref, coefs_ref, weights_hbm, angles_ref, cot_ref,
    atom_ref, coef_ref, spread_ref, left_ref, both_hbm, back_hbm, cot_hbm,
    feats, weights, merged, mine, crystal, cots, x_all, both_all, back_all, coef_parts, wide,
    x_parts, x_pair, x_held, x_slots, x_cross, out_parts, out_pair, out_held, out_slots, out_cross,
    load_sem, weight_sem, store_sem, send_sem, recv_sem,
):
    d, m = lax.axis_index("dp"), lax.axis_index("mp")
    z, y, x, core = d // 2, m // 8 * 2 + d % 2, m // 2 % 4, m % 2
    y_hi, y_lo = m // 8, d % 2
    tiles, experts, double, _ = weights.shape
    rows, width = double // 2, tiles * LANES
    other = 1 - core
    ahead, behind, far = (x + 1) % 4, (x + 3) % 4, (x + 2) % 4

    def device(z, y, x, core):
        return (z * 2 + y % 2, y // 2 * 8 + x * 2 + core)

    sibling = device(z, y, x, other)
    x_next, x_last = device(z, y, ahead, core), device(z, y, behind, core)
    y_peer = device(z, (y + 2) % 4, x, core)
    x_far, z_far = device(z, y, far, core), device((z + 2) % 4, y, x, core)
    z_next, z_last = device((z + 1) % 4, y, x, core), device((z + 3) % 4, y, x, core)
    y_next, y_last = device(z, (y + 1) % 4, x, core), device(z, (y + 3) % 4, x, core)
    lo_peer = (d + 1 - 2 * y_lo, m)

    def mp_peer(j):
        return (d, lax.rem(m + j, MP))

    def span(start, stop, body):
        lax.fori_loop(start, stop, lambda j, c: (body(j), c)[1], 0)

    barrier = pltpu.get_barrier_semaphore()
    span(1, MP, lambda j: pl.semaphore_signal(barrier, inc=1, device_id=mp_peer(j), device_id_type=MESH))
    for to in (z_next, z_last, z_far, y_next, y_last):
        pl.semaphore_signal(barrier, inc=1, device_id=to, device_id_type=MESH)

    feats_copy = pltpu.make_async_copy(feats_hbm, feats, load_sem)
    feats_copy.start()
    weight_rows = weights_hbm.reshape(experts, double, width)

    def weight_copy(t):
        cols = pl.ds(pl.multiple_of(t * LANES, LANES), LANES)
        return pltpu.make_async_copy(weight_rows.at[:, :, cols], weights.at[t], weight_sem.at[t])

    span(0, tiles, lambda t: weight_copy(t).start())

    sent = []

    def send(sem, src, dst, to):
        copy = remote(src, dst, send_sem.at[sem], recv_sem.at[sem], to)
        copy.start()
        sent.append(copy)

    def arrive(sem, ref):
        remote(ref, ref, send_sem.at[sem], recv_sem.at[sem], sibling).wait_recv()

    c = cot_ref[...].astype(F32)
    own = jnp.concatenate([c[:, :width], c[:, width:]], 0).astype(BF16)
    crystal[y_hi, x, core] = own
    for s in range(SLICES):
        mine[s] = own[:, s * COLS : (s + 1) * COLS]
    for o in range(3):
        cots[3 * core + o, z, y, x, core] = mine[3 * core + o]

    slots = targets_ref.shape[1]
    table = rolls_ref[...] == lax.broadcasted_iota(jnp.int32, (angles_ref.shape[1], slots), 0)
    angle = column_of(angles_ref[...])
    valid = lax.broadcasted_iota(jnp.int32, (1, slots), 1) < counts_ref[0]
    factor = jnp.where(valid, scale, 0.0)
    cosine = column_of(jnp.sum(jnp.where(table, jnp.cos(angle), 0.0), 0, keepdims=True) * factor)
    sine = column_of(jnp.sum(jnp.where(table, jnp.sin(angle), 0.0), 0, keepdims=True) * factor)
    target = column_of(targets_ref[...].astype(F32)).astype(jnp.int32)
    q = lax.broadcasted_iota(jnp.int32, (slots, spread_ref.shape[2]), 1)
    hit = target == q // 16 * 8 + q % 8
    real = q // 8 % 2 == 0
    spread_ref[0] = jnp.where(hit, jnp.where(real, cosine, sine), 0.0).astype(BF16)
    spread_ref[1] = jnp.where(hit, jnp.where(real, -sine, cosine), 0.0).astype(BF16)

    pl.semaphore_wait(barrier, MP - 1 + 5)

    theirs = pl.ds(3 * other, 3)
    send(SWAP, mine.at[theirs], cots.at[theirs, z, y, x, core], sibling)

    here = {"z": z, "y": y, "x": x}
    nexts = {"z": (z_next, z_last, z_far), "y": (y_next, y_last, y_peer), "x": (x_next, x_last, x_far)}

    def region(o, stage, by, whose):
        order = ORDERS[o]
        index = dict(here)
        for a in order[:stage]:
            index[a] = slice(None)
        index[order[stage]] = (here[order[stage]] + by) % 4
        return cots.at[3 * whose + o, index["z"], index["y"], index["x"]]

    def ring_send(stage):
        for o in range(3):
            ref = region(o, stage, 0, core)
            for i, to in enumerate(nexts[ORDERS[o][stage]]):
                send(RING + (o * 3 + stage) * 3 + i, ref, ref, to)

    def ring_arrive(o, stage, i):
        arrive(RING + (o * 3 + stage) * 3 + i, region(o, stage, (3, 1, 2)[i], core))

    def ring_all(stage):
        for o in range(3):
            for i in range(3):
                ring_arrive(o, stage, i)

    def plane_send(o, by):
        ref = region(o, 2, by, core)
        send(PLANE + o * 4 + by, ref, ref, sibling)

    def plane_arrive(o, by):
        arrive(PLANE + o * 4 + by, region(o, 2, by, other))

    low = 1 - y_hi
    along = ((x_next, ahead), (x_last, behind), (x_far, far))

    def sum_cores(base, parts, pair):
        send(base, parts.at[other], pair, sibling)

    def sum_x(base, parts, pair, held, slots):
        arrive(base, pair)
        for n, h in enumerate((low, y_hi)):
            for i in range(4):
                held[i, h] = (parts[core, h, i].astype(F32) + pair[h, i].astype(F32)).astype(BF16)
            for i, (to, at) in enumerate(along):
                send(base + 1 + 3 * n + i, held.at[at, h], slots.at[n, i], to)

    def sum_of(base, held, slots, n, h):
        total = held[x, h].astype(F32)
        for i in range(3):
            arrive(base + 1 + 3 * n + i, slots.at[n, i])
            total += slots[n, i].astype(F32)
        return total

    def sum_y(base, held, slots, cross):
        cross[0] = sum_of(base, held, slots, 0, low).astype(BF16)
        send(base + 7, cross.at[0], cross.at[1], y_peer)

    def sum_end(base, held, slots, cross):
        total = sum_of(base, held, slots, 1, y_hi)
        arrive(base + 7, cross.at[1])
        return total + cross[1].astype(F32)

    def gather_first(base, ref):
        own = ref.at[y_hi, x, core]
        for i, to in enumerate((y_peer, x_next, x_last, x_far)):
            send(base + i, own, own, to)

    def gather_second(base, ref):
        got = ref.at[low, x, core]
        arrive(base, got)
        for i, (to, _) in enumerate(along):
            send(base + 4 + i, got, got, to)

    def gather_cores(base, ref):
        for n, h in enumerate((y_hi, low)):
            for i, at in enumerate((behind, ahead, far)):
                arrive(base + 1 + 3 * n + i, ref.at[h, at, core])
        ours = ref.at[:, :, core]
        send(base + 7, ours, ours, sibling)

    def gather_end(base, ref):
        arrive(base + 7, ref.at[:, :, other])

    gather_first(COT, crystal)

    feats_copy.wait()
    group = 4
    block = group * rows

    def spread_block(i):
        plus = feats[:, pl.ds(pl.multiple_of(i * block, block), block)]
        minus = feats[:, pl.ds(pl.multiple_of(width + i * block, block), block)]
        part = dot(plus, spread_ref[0], ((0,), (0,))) + dot(minus, spread_ref[1], ((0,), (0,)))
        part = part.astype(BF16)
        for g in range(group):
            x_parts[g % 2, i // 2, i % 2 * 2 + g // 2] = part[g * rows : (g + 1) * rows]

    span(0, width // block, spread_block)
    sum_cores(X_SUM, x_parts, x_pair)
    arrive(SWAP, cots.at[pl.ds(3 * core, 3), z, y, x, other])
    ring_send(0)
    sum_x(X_SUM, x_parts, x_pair, x_held, x_slots)
    gather_second(COT, crystal)

    def merge(t):
        weight_copy(t).wait()
        total = jnp.zeros((double, LANES), F32)
        for k in range(experts):
            total += coefs_ref[d, k] * weights[t, k].astype(F32)
        merged[:, pl.ds(pl.multiple_of(t * LANES, LANES), LANES)] = total.astype(BF16)

    span(0, tiles // 3, merge)
    ring_all(0)
    ring_send(1)
    sum_y(X_SUM, x_held, x_slots, x_cross)
    span(tiles // 3, 2 * tiles // 3, merge)
    gather_cores(COT, crystal)
    span(2 * tiles // 3, tiles, merge)

    gather_end(COT, crystal)
    by_real, by_imag = separate(wide, dot(merged[...], crystal[...].reshape(-1, width), ((1,), (1,))))
    back_all[y_hi, x, core] = (by_real + turn(by_imag)).astype(BF16)
    gather_first(BACK, back_all)

    x_here = sum_end(X_SUM, x_held, x_slots, x_cross).astype(BF16)
    x_all[d] = x_here
    send(X_DP, x_all.at[d], x_all.at[d], lo_peer)
    x_wide = x_here.astype(F32)
    both = interleave(wide, x_wide, -turn(x_wide))
    both_turned = both.T.astype(BF16)
    both = both.astype(BF16)

    def out_block(i):
        cols = pl.ds(pl.multiple_of(i * block, block), block)
        part = dot(both_turned, merged[:, cols], ((1,), (0,))).astype(BF16)
        for p in range(MP):
            out_parts[p % 2, p // 8, p // 2 % 4, :, cols] = part[p * 16 : (p + 1) * 16]

    span(0, width // block, out_block)
    sum_cores(OUT_SUM, out_parts, out_pair)

    ring_all(1)
    ring_send(2)
    for o in range(3):
        plane_send(o, 0)
    gather_second(BACK, back_all)
    sum_x(OUT_SUM, out_parts, out_pair, out_held, out_slots)
    pair = x_all.at[pl.ds(2 * z, 2)]
    arrive(X_DP, x_all.at[d + 1 - 2 * y_lo])
    for i, to in enumerate((z_next, z_last, z_far)):
        send(X_DP + 1 + i, pair, pair, to)

    def coef_add(t, sums):
        cols = pl.ds(pl.multiple_of(t * LANES, LANES), LANES)
        grad = dot(both, crystal[:, :, :, :, cols].reshape(-1, LANES), ((1,), (0,))) * norm
        added = []
        for k in range(experts):
            terms = weights[t, k].astype(F32) * grad
            added.append(sums[k] + jnp.sum(terms.reshape(-1, 8, LANES), 0))
        return tuple(added)

    sums = tuple(jnp.zeros((8, LANES), F32) for _ in range(experts))
    sums = lax.fori_loop(0, tiles // 2, coef_add, sums)
    sum_y(OUT_SUM, out_held, out_slots, out_cross)
    sums = lax.fori_loop(tiles // 2, tiles, coef_add, sums)
    lanes = jnp.sum(jnp.concatenate([jnp.sum(v, 0, keepdims=True) for v in sums], 0), 1, keepdims=True)
    same = lax.broadcasted_iota(jnp.int32, (experts, LANES), 0) == lax.broadcasted_iota(
        jnp.int32, (experts, LANES), 1
    )
    coef_parts[0] = jnp.sum(jnp.where(same, lanes, 0.0), 0, keepdims=True)

    def coef_copy(j):
        sem = COEF + j - 1
        return remote(coef_parts.at[0], coef_parts.at[j], send_sem.at[sem], recv_sem.at[sem], mp_peer(j))

    span(1, MP, lambda j: coef_copy(j).start())

    gather_cores(BACK, back_all)

    r = lax.broadcasted_iota(jnp.int32, (32, 32 * DP), 0)
    c = lax.broadcasted_iota(jnp.int32, (32, 32 * DP), 1)
    for k in range(experts):
        row = jnp.zeros((32, 32 * DP), F32)
        for i in range(DP):
            row = jnp.where(c == r + 32 * i, coefs_ref[i, k], row)
        left_ref[k * 32 : (k + 1) * 32] = row.astype(BF16)

    out = sum_end(OUT_SUM, out_held, out_slots, out_cross)
    half = out.shape[0] // 2
    atom_ref[...] = jnp.concatenate([out[:half], out[half:]], 1).astype(BF16)

    for by, i in ((3, 0), (1, 1), (2, 2)):
        arrive(X_DP + 1 + i, x_all.at[pl.ds((z + by) % 4 * 2, 2)])
    for i in range(DP):
        rows_of = x_all[i].astype(F32)
        both_all[i] = interleave(wide, rows_of, -turn(rows_of)).astype(BF16)

    stores = []

    def store(src, dst):
        copy = pltpu.make_async_copy(src, dst, store_sem.at[len(stores)])
        copy.start()
        stores.append(copy)

    store(both_all, both_hbm)
    gather_end(BACK, back_all)
    store(back_all, back_hbm)
    for i, by in enumerate((3, 1, 2)):
        for o in range(3):
            ring_arrive(o, 2, i)
            plane_send(o, by)
    for o in range(3):
        store(cots.at[3 * core + o], cot_hbm.at[3 * core + o])

    span(1, MP, lambda j: coef_copy(j).wait_recv())
    coef_ref[...] = jnp.sum(coef_parts[...], 0)[:, :experts] * (width**-0.5)

    for by in (0, 3, 1, 2):
        for o in range(3):
            plane_arrive(o, by)
            index = [slice(None)] * 3
            axis = "zyx".index(ORDERS[o][2])
            index[axis] = (here["zyx"[axis]] + by) % 4
            at = (3 * other + o, *index)
            store(cots.at[at], cot_hbm.at[at])

    span(1, MP, lambda j: coef_copy(j).wait_send())
    for copy in sent:
        copy.wait_send()
    for copy in stores:
        copy.wait()


def exchange(edge_feats, targets, roll_ids, counts, coefs, weights, roll_angles, atom_cot):
    slots, wide = edge_feats.shape
    width = wide // 2
    experts, rows = weights.shape[:2]
    atoms_here = atom_cot.shape[0]
    q = 2 * MP * atoms_here
    vmem = pl.BlockSpec(memory_space=pltpu.VMEM)
    smem = pl.BlockSpec(memory_space=pltpu.SMEM)
    hbm = pl.BlockSpec(memory_space=pl.ANY)
    dma = pltpu.SemaphoreType.DMA
    cots = (SLICES, 4, 4, 4, 2, 16, COLS)
    sums = [
        pltpu.VMEM(lead + block, BF16)
        for block in ((rows, q), (16, width))
        for lead in ((2, 2, 4), (2, 4), (4, 2), (2, 3), (2,))
    ]
    return pl.pallas_call(
        functools.partial(exchange_kernel, (atoms_here / slots) ** 0.5, (slots * MP) ** -0.5),
        in_specs=[hbm, vmem, vmem, smem, smem, hbm, vmem, vmem],
        out_specs=[vmem, vmem, vmem, vmem, hbm, hbm, hbm],
        out_shape=[
            jax.ShapeDtypeStruct(atom_cot.shape, BF16),
            jax.ShapeDtypeStruct((1, experts), F32),
            jax.ShapeDtypeStruct((2, slots, q), BF16),
            jax.ShapeDtypeStruct((32 * experts, 32 * DP), BF16),
            jax.ShapeDtypeStruct((DP, 2 * rows, q), BF16),
            jax.ShapeDtypeStruct((2, 4, 2, rows, q), BF16),
            jax.ShapeDtypeStruct(cots, BF16),
        ],
        scratch_shapes=[
            pltpu.VMEM(edge_feats.shape, BF16),
            pltpu.VMEM((width // LANES, experts, 2 * rows, LANES), BF16),
            pltpu.VMEM((2 * rows, width), BF16),
            pltpu.VMEM((SLICES, 16, COLS), BF16),
            pltpu.VMEM((2, 4, 2, 16, width), BF16),
            pltpu.VMEM(cots, BF16),
            pltpu.VMEM((DP, rows, q), BF16),
            pltpu.VMEM((DP, 2 * rows, q), BF16),
            pltpu.VMEM((2, 4, 2, rows, q), BF16),
            pltpu.VMEM((MP, 1, LANES), F32),
            pltpu.VMEM((2, 2 * rows, LANES), F32),
            *sums,
            dma(()), dma((width // LANES,)), dma((17,)), dma((COPIES,)), dma((COPIES,)),
        ],
        compiler_params=pltpu.CompilerParams(
            collective_id=0, has_side_effects=True, vmem_limit_bytes=56 * 2**20
        ),
        cost_estimate=pl.CostEstimate(flops=4 * 10**9, bytes_accessed=2 * 10**7, transcendentals=0),
    )(
        edge_feats, targets[None], roll_ids[None], counts, coefs, weights, roll_angles[None], atom_cot
    )


def mix_kernel(norm, left_ref, both_ref, cot_ref, back_ref, spread_ref, wg_hbm, eg_ref, gm_ref, out_ref, sem):
    step, steps = pl.program_id(0), pl.num_programs(0)
    crystals, double, _ = both_ref.shape
    experts, _, _, width = wg_hbm.shape
    wg_rows = wg_hbm.reshape(experts, double, width)

    for i in range(crystals):
        cot = jnp.concatenate(
            [cot_ref[0, i // 2, i % 2 + 2 * h].reshape(LANES, COLS) for h in range(2)], 0
        )
        gm_ref[i] = (dot(both_ref[i], cot, ((1,), (0,))) * norm).astype(BF16)

    slot = lax.rem(step, 2)

    def copies(step):
        slot = lax.rem(step, 2)
        return [
            pltpu.make_async_copy(
                out_ref.at[slot, t],
                wg_rows.at[:, :, pl.ds(pl.multiple_of(step * COLS + t * LANES, LANES), LANES)],
                sem.at[slot, t],
            )
            for t in range(2)
        ]

    @pl.when(step >= 2)
    def _():
        for copy in copies(step - 2):
            copy.wait()

    for g in range(double // 32):
        right = jnp.concatenate([gm_ref[i, g * 32 : (g + 1) * 32, :] for i in range(crystals)], 0)
        out = dot(left_ref[...], right, ((1,), (0,))).astype(BF16)
        for t in range(2):
            for k in range(experts):
                piece = out[k * 32 : (k + 1) * 32, t * LANES : (t + 1) * LANES]
                out_ref[slot, t, k, g * 32 : (g + 1) * 32] = piece

    for copy in copies(step):
        copy.start()

    part = step // (steps // 2)
    cols = eg_ref.shape[1]
    at = pl.multiple_of(step % (steps // 2) * cols, cols)
    eg_ref[...] = dot(spread_ref[part], back_ref[pl.ds(at, cols), :], ((1,), (1,))).astype(BF16)

    @pl.when(step == steps - 1)
    def _():
        for copy in copies(step - 1) + copies(step):
            copy.wait()


def mix(experts, left, both_all, cot_all, back_all, spread, norm):
    crystals, double, _ = both_all.shape
    width = back_all.shape[0]
    slots = spread.shape[1]
    whole = lambda shape: pl.BlockSpec(shape, lambda i: (0,) * len(shape))
    return pl.pallas_call(
        functools.partial(mix_kernel, norm),
        grid=(SLICES,),
        in_specs=[
            whole(left.shape),
            whole(both_all.shape),
            pl.BlockSpec((1,) + cot_all.shape[1:], lambda i: (i,) + (0,) * 6),
            whole(back_all.shape),
            whole(spread.shape),
        ],
        out_specs=[
            pl.BlockSpec(memory_space=pl.ANY),
            pl.BlockSpec((slots, 2 * width // SLICES), lambda i: (0, i)),
        ],
        out_shape=[
            jax.ShapeDtypeStruct((experts, double // 2, 2, width), BF16),
            jax.ShapeDtypeStruct((slots, 2 * width), BF16),
        ],
        scratch_shapes=[
            pltpu.VMEM((crystals, double, COLS), BF16),
            pltpu.VMEM((2, 2, experts, double, LANES), BF16),
            pltpu.SemaphoreType.DMA((2, 2)),
        ],
        compiler_params=pltpu.CompilerParams(vmem_limit_bytes=60 * 2**20),
        cost_estimate=pl.CostEstimate(flops=10**10, bytes_accessed=2 * 10**7, transcendentals=0),
    )(left, both_all, cot_all, back_all, spread)


def on_device(edge_feats, targets, roll_ids, counts, coefs, weights, roll_angles, atom_cot):
    slots = edge_feats.shape[0]
    atom_out, coef_grad, spread, left, both_all, back_all, cot_all = exchange(
        edge_feats, targets, roll_ids, counts, coefs, weights, roll_angles, atom_cot
    )
    back_all = back_all.reshape(-1, back_all.shape[-1])
    weight_grad, edge_grad = mix(
        weights.shape[0], left, both_all, cot_all, back_all, spread, (slots * MP) ** -0.5
    )
    return (atom_out, edge_grad, weight_grad, coef_grad)


def solution(mesh):
    placed = (
        P(("dp", "mp"), None),
        P(("dp", "mp")),
        P(("dp", "mp")),
        P(("dp", "mp")),
        P(),
        P(None, "mp", None, None),
        P(),
        P(("dp", "mp"), None),
    )
    return jax.shard_map(
        on_device,
        mesh=mesh,
        in_specs=placed,
        out_specs=(
            P(("dp", "mp"), None),
            P(("dp", "mp"), None),
            P(None, "mp", None, None),
            P("dp", None),
        ),
        check_vma=False,
    )
```

```python
import functools

import jax
import jax.numpy as jnp
from jax import lax
from jax.experimental import pallas as pl
from jax.experimental.pallas import tpu as pltpu
from jax.sharding import PartitionSpec as P

BF16, F32 = jnp.bfloat16, jnp.float32
LANES = 128
MESH = pl.DeviceIdType.MESH
DP, MP = 8, 16
SLICES, COLS = 6, 256
FLOWS = ((0, "xyz"), (1, "zxy"), (2, "yzx"))
SWAP, RING, PLANE, X_SUM, OUT_SUM, COT, BACK, X_DP, COEF = 0, 1, 28, 40, 48, 56, 64, 72, 76
COPIES = COEF + MP - 1


def dot(a, b, contract):
    return lax.dot_general(a, b, (contract, ((), ())), preferred_element_type=F32)


def turn(rows):
    n = rows.shape[1]
    col = lax.broadcasted_iota(jnp.int32, rows.shape, 1)
    return jnp.where(col // 8 % 2 == 0, pltpu.roll(rows, n - 8, 1), -pltpu.roll(rows, 8, 1))


def interleave(wide, even, odd):
    n = even.shape[0]
    for h in range(2):
        wide[h, pl.ds(0, n, stride=2), :] = even[:, h * LANES : (h + 1) * LANES]
        wide[h, pl.ds(1, n, stride=2), :] = odd[:, h * LANES : (h + 1) * LANES]
    return jnp.concatenate([wide[0], wide[1]], 1)


def separate(wide, both):
    n = both.shape[0] // 2
    for h in range(2):
        wide[h] = both[:, h * LANES : (h + 1) * LANES]
    return [
        jnp.concatenate([wide[h, pl.ds(part, n, stride=2), :] for h in range(2)], 1) for part in range(2)
    ]


def remote(src, dst, send, recv, target):
    return pltpu.make_async_remote_copy(
        src_ref=src, dst_ref=dst, send_sem=send, recv_sem=recv, device_id=target, device_id_type=MESH
    )


def column_of(row):
    n = row.shape[1]
    same = lax.broadcasted_iota(jnp.int32, (n, n), 0) == lax.broadcasted_iota(jnp.int32, (n, n), 1)
    return jnp.sum(jnp.where(same, row, 0.0), 1, keepdims=True)


def exchange_kernel(
    scale, norm,
    feats_hbm, targets_ref, rolls_ref, counts_ref, coefs_ref, weights_hbm, angles_ref, cot_ref,
    atom_ref, coef_ref, spread_ref, left_ref, both_hbm, back_hbm, cot_hbm,
    feats, weights, merged, mine, crystal, cots, x_all, both_all, back_all, coef_parts, wide,
    x_parts, x_pair, x_held, x_slots, x_cross, out_parts, out_pair, out_held, out_slots, out_cross,
    load_sem, weight_sem, store_sem, send_sem, recv_sem,
):
    d, m = lax.axis_index("dp"), lax.axis_index("mp")
    z, y, x, core = d // 2, m // 8 * 2 + d % 2, m // 2 % 4, m % 2
    y_hi, y_lo = m // 8, d % 2
    tiles, experts, double, _ = weights.shape
    rows, width = double // 2, tiles * LANES
    other = 1 - core
    ahead, behind, far = (x + 1) % 4, (x + 3) % 4, (x + 2) % 4

    def device(z, y, x, core):
        return (z * 2 + y % 2, y // 2 * 8 + x * 2 + core)

    sibling = device(z, y, x, other)
    x_next, x_last = device(z, y, ahead, core), device(z, y, behind, core)
    y_peer = device(z, (y + 2) % 4, x, core)
    x_far, z_far = device(z, y, far, core), device((z + 2) % 4, y, x, core)
    z_next, z_last = device((z + 1) % 4, y, x, core), device((z + 3) % 4, y, x, core)
    y_next, y_last = device(z, (y + 1) % 4, x, core), device(z, (y + 3) % 4, x, core)
    lo_peer = (d + 1 - 2 * y_lo, m)

    def mp_peer(j):
        return (d, lax.rem(m + j, MP))

    def span(start, stop, body):
        lax.fori_loop(start, stop, lambda j, c: (body(j), c)[1], 0)

    barrier = pltpu.get_barrier_semaphore()
    span(1, MP, lambda j: pl.semaphore_signal(barrier, inc=1, device_id=mp_peer(j), device_id_type=MESH))
    for to in (z_next, z_last, z_far, y_next, y_last):
        pl.semaphore_signal(barrier, inc=1, device_id=to, device_id_type=MESH)

    feats_copy = pltpu.make_async_copy(feats_hbm, feats, load_sem)
    feats_copy.start()
    weight_rows = weights_hbm.reshape(experts, double, width)

    def weight_copy(t):
        cols = pl.ds(pl.multiple_of(t * LANES, LANES), LANES)
        return pltpu.make_async_copy(weight_rows.at[:, :, cols], weights.at[t], weight_sem.at[t])

    span(0, tiles, lambda t: weight_copy(t).start())

    sent = []

    def send(sem, src, dst, to):
        copy = remote(src, dst, send_sem.at[sem], recv_sem.at[sem], to)
        copy.start()
        sent.append(copy)

    def arrive(sem, ref):
        remote(ref, ref, send_sem.at[sem], recv_sem.at[sem], sibling).wait_recv()

    c = cot_ref[...].astype(F32)
    own = jnp.concatenate([c[:, :width], c[:, width:]], 0).astype(BF16)
    crystal[y_hi, x, core] = own
    for s in range(SLICES):
        mine[s] = own[:, s * COLS : (s + 1) * COLS]
    for o in range(3):
        cots[3 * core + o, z, y, x, core] = mine[3 * core + o]

    slots = targets_ref.shape[1]
    table = rolls_ref[...] == lax.broadcasted_iota(jnp.int32, (angles_ref.shape[1], slots), 0)
    angle = column_of(angles_ref[...])
    valid = lax.broadcasted_iota(jnp.int32, (1, slots), 1) < counts_ref[0]
    factor = jnp.where(valid, scale, 0.0)
    cosine = column_of(jnp.sum(jnp.where(table, jnp.cos(angle), 0.0), 0, keepdims=True) * factor)
    sine = column_of(jnp.sum(jnp.where(table, jnp.sin(angle), 0.0), 0, keepdims=True) * factor)
    target = column_of(targets_ref[...].astype(F32)).astype(jnp.int32)
    q = lax.broadcasted_iota(jnp.int32, (slots, spread_ref.shape[2]), 1)
    hit = target == q // 16 * 8 + q % 8
    real = q // 8 % 2 == 0
    spread_ref[0] = jnp.where(hit, jnp.where(real, cosine, sine), 0.0).astype(BF16)
    spread_ref[1] = jnp.where(hit, jnp.where(real, -sine, cosine), 0.0).astype(BF16)

    pl.semaphore_wait(barrier, MP - 1 + 5)

    theirs = pl.ds(3 * other, 3)
    send(SWAP, mine.at[theirs], cots.at[theirs, z, y, x, core], sibling)

    here = {"z": z, "y": y, "x": x}
    nexts = {"z": (z_next, z_last, z_far), "y": (y_next, y_last, y_peer), "x": (x_next, x_last, x_far)}

    def region(o, stage, by, whose, ref=cots):
        order = FLOWS[o][1]
        index = dict(here)
        for a in order[:stage]:
            index[a] = slice(None)
        index[order[stage]] = (here[order[stage]] + by) % 4
        return ref.at[3 * whose + o, index["z"], index["y"], index["x"]]

    def ring_send(stage, which=(0, 1, 2), ways=(0, 1, 2)):
        for o in which:
            ref = region(o, stage, 0, core)
            for i in ways:
                send(RING + (o * 3 + stage) * 3 + i, ref, ref, nexts[FLOWS[o][1][stage]][i])

    def ring_arrive(o, stage, i):
        arrive(RING + (o * 3 + stage) * 3 + i, region(o, stage, (3, 1, 2)[i], core))

    def ring_all(stage):
        for o in range(3):
            for i in range(3):
                ring_arrive(o, stage, i)

    stores = []

    def store(src, dst):
        copy = pltpu.make_async_copy(src, dst, store_sem.at[len(stores)])
        copy.start()
        stores.append(copy)

    def plane_send(o, by):
        src, dst = region(o, 2, by, core), region(o, 2, by, core, cot_hbm)
        send(PLANE + o * 4 + by, src, dst, sibling)
        store(src, dst)

    def plane_arrive(o, by):
        arrive(PLANE + o * 4 + by, region(o, 2, by, other, cot_hbm))

    low = 1 - y_hi
    along = ((x_next, ahead), (x_last, behind), (x_far, far))

    def sum_cores(base, parts, pair):
        send(base, parts.at[other], pair, sibling)

    def sum_x(base, parts, pair, held, slots):
        arrive(base, pair)
        for n, h in enumerate((low, y_hi)):
            for i in range(4):
                held[i, h] = (parts[core, h, i].astype(F32) + pair[h, i].astype(F32)).astype(BF16)
            for i, (to, at) in enumerate(along):
                send(base + 1 + 3 * n + i, held.at[at, h], slots.at[n, i], to)

    def sum_of(base, held, slots, n, h):
        total = held[x, h].astype(F32)
        for i in range(3):
            arrive(base + 1 + 3 * n + i, slots.at[n, i])
            total += slots[n, i].astype(F32)
        return total

    def sum_y(base, held, slots, cross):
        cross[0] = sum_of(base, held, slots, 0, low).astype(BF16)
        send(base + 7, cross.at[0], cross.at[1], y_peer)

    def sum_end(base, held, slots, cross):
        total = sum_of(base, held, slots, 1, y_hi)
        arrive(base + 7, cross.at[1])
        return total + cross[1].astype(F32)

    def gather_first(base, ref):
        own = ref.at[y_hi, x, core]
        for i, to in enumerate((y_peer, x_next, x_last, x_far)):
            send(base + i, own, own, to)

    def gather_second(base, ref):
        got = ref.at[low, x, core]
        arrive(base, got)
        for i, (to, _) in enumerate(along):
            send(base + 4 + i, got, got, to)

    def gather_cores(base, ref):
        for n, h in enumerate((y_hi, low)):
            for i, at in enumerate((behind, ahead, far)):
                arrive(base + 1 + 3 * n + i, ref.at[h, at, core])
        ours = ref.at[:, :, core]
        send(base + 7, ours, ours, sibling)

    def gather_end(base, ref):
        arrive(base + 7, ref.at[:, :, other])

    gather_first(COT, crystal)
    arrive(SWAP, cots.at[pl.ds(3 * core, 3), z, y, x, other])
    ring_send(0)

    feats_copy.wait()
    group = 4
    block = group * rows

    def spread_block(i):
        plus = feats[:, pl.ds(pl.multiple_of(i * block, block), block)]
        minus = feats[:, pl.ds(pl.multiple_of(width + i * block, block), block)]
        part = dot(plus, spread_ref[0], ((0,), (0,))) + dot(minus, spread_ref[1], ((0,), (0,)))
        part = part.astype(BF16)
        for g in range(group):
            x_parts[g % 2, i // 2, i % 2 * 2 + g // 2] = part[g * rows : (g + 1) * rows]

    span(0, width // block, spread_block)
    sum_cores(X_SUM, x_parts, x_pair)
    sum_x(X_SUM, x_parts, x_pair, x_held, x_slots)
    gather_second(COT, crystal)
    ring_all(0)
    ring_send(1)

    def merge(t):
        weight_copy(t).wait()
        total = jnp.zeros((double, LANES), F32)
        for k in range(experts):
            total += coefs_ref[d, k] * weights[t, k].astype(F32)
        merged[:, pl.ds(pl.multiple_of(t * LANES, LANES), LANES)] = total.astype(BF16)

    span(0, 2 * tiles // 3, merge)
    sum_y(X_SUM, x_held, x_slots, x_cross)
    span(2 * tiles // 3, tiles, merge)
    ring_all(1)
    ring_send(2, (0,))
    gather_cores(COT, crystal)
    x_here = sum_end(X_SUM, x_held, x_slots, x_cross).astype(BF16)
    x_all[d] = x_here
    send(X_DP, x_all.at[d], x_all.at[d], lo_peer)
    x_wide = x_here.astype(F32)
    both = interleave(wide, x_wide, -turn(x_wide))
    both_turned = both.T.astype(BF16)
    both = both.astype(BF16)

    def out_block(i):
        cols = pl.ds(pl.multiple_of(i * block, block), block)
        part = dot(both_turned, merged[:, cols], ((1,), (0,))).astype(BF16)
        for p in range(MP):
            out_parts[p % 2, p // 8, p // 2 % 4, :, cols] = part[p * 16 : (p + 1) * 16]

    span(0, width // block, out_block)
    sum_cores(OUT_SUM, out_parts, out_pair)

    gather_end(COT, crystal)
    by_real, by_imag = separate(wide, dot(merged[...], crystal[...].reshape(-1, width), ((1,), (1,))))
    back_all[y_hi, x, core] = (by_real + turn(by_imag)).astype(BF16)
    gather_first(BACK, back_all)
    sum_x(OUT_SUM, out_parts, out_pair, out_held, out_slots)
    ring_send(2, (1,), (0, 1))
    gather_second(BACK, back_all)
    ring_send(2, (2,))
    for o in range(3):
        plane_send(o, 0)
    pair = x_all.at[pl.ds(2 * z, 2)]
    arrive(X_DP, x_all.at[d + 1 - 2 * y_lo])
    for i, to in enumerate((z_next, z_last, z_far)):
        send(X_DP + 1 + i, pair, pair, to)

    def coef_add(t, sums):
        cols = pl.ds(pl.multiple_of(t * LANES, LANES), LANES)
        grad = dot(both, crystal[:, :, :, :, cols].reshape(-1, LANES), ((1,), (0,))) * norm
        added = []
        for k in range(experts):
            terms = weights[t, k].astype(F32) * grad
            added.append(sums[k] + jnp.sum(terms.reshape(-1, 8, LANES), 0))
        return tuple(added)

    sums = tuple(jnp.zeros((8, LANES), F32) for _ in range(experts))
    sums = lax.fori_loop(0, tiles // 2, coef_add, sums)
    sum_y(OUT_SUM, out_held, out_slots, out_cross)
    ring_send(2, (1,), (2,))
    sums = lax.fori_loop(tiles // 2, tiles, coef_add, sums)
    lanes = jnp.sum(jnp.concatenate([jnp.sum(v, 0, keepdims=True) for v in sums], 0), 1, keepdims=True)
    same = lax.broadcasted_iota(jnp.int32, (experts, LANES), 0) == lax.broadcasted_iota(
        jnp.int32, (experts, LANES), 1
    )
    coef_parts[0] = jnp.sum(jnp.where(same, lanes, 0.0), 0, keepdims=True)

    def coef_copy(j):
        sem = COEF + j - 1
        return remote(coef_parts.at[0], coef_parts.at[j], send_sem.at[sem], recv_sem.at[sem], mp_peer(j))

    span(1, MP, lambda j: coef_copy(j).start())

    gather_cores(BACK, back_all)

    r = lax.broadcasted_iota(jnp.int32, (32, 32 * DP), 0)
    c = lax.broadcasted_iota(jnp.int32, (32, 32 * DP), 1)
    for k in range(experts):
        row = jnp.zeros((32, 32 * DP), F32)
        for i in range(DP):
            row = jnp.where(c == r + 32 * i, coefs_ref[i, k], row)
        left_ref[k * 32 : (k + 1) * 32] = row.astype(BF16)

    out = sum_end(OUT_SUM, out_held, out_slots, out_cross)
    half = out.shape[0] // 2
    atom_ref[...] = jnp.concatenate([out[:half], out[half:]], 1).astype(BF16)

    for by, i in ((3, 0), (1, 1), (2, 2)):
        arrive(X_DP + 1 + i, x_all.at[pl.ds((z + by) % 4 * 2, 2)])
    for i in range(DP):
        rows_of = x_all[i].astype(F32)
        both_all[i] = interleave(wide, rows_of, -turn(rows_of)).astype(BF16)

    store(both_all, both_hbm)
    gather_end(BACK, back_all)
    store(back_all, back_hbm)
    for i, by in enumerate((3, 1, 2)):
        for o in range(3):
            ring_arrive(o, 2, i)
            plane_send(o, by)
    span(1, MP, lambda j: coef_copy(j).wait_recv())
    coef_ref[...] = jnp.sum(coef_parts[...], 0)[:, :experts] * (width**-0.5)

    for by in (0, 3, 1, 2):
        for o in range(3):
            plane_arrive(o, by)

    span(1, MP, lambda j: coef_copy(j).wait_send())
    for copy in sent:
        copy.wait_send()
    for copy in stores:
        copy.wait()


def exchange(edge_feats, targets, roll_ids, counts, coefs, weights, roll_angles, atom_cot):
    slots, wide = edge_feats.shape
    width = wide // 2
    experts, rows = weights.shape[:2]
    atoms_here = atom_cot.shape[0]
    q = 2 * MP * atoms_here
    vmem = pl.BlockSpec(memory_space=pltpu.VMEM)
    smem = pl.BlockSpec(memory_space=pltpu.SMEM)
    hbm = pl.BlockSpec(memory_space=pl.ANY)
    dma = pltpu.SemaphoreType.DMA
    cots = (SLICES, 4, 4, 4, 2, 16, COLS)
    sums = [
        pltpu.VMEM(lead + block, BF16)
        for block in ((rows, q), (16, width))
        for lead in ((2, 2, 4), (2, 4), (4, 2), (2, 3), (2,))
    ]
    return pl.pallas_call(
        functools.partial(exchange_kernel, (atoms_here / slots) ** 0.5, (slots * MP) ** -0.5),
        in_specs=[hbm, vmem, vmem, smem, smem, hbm, vmem, vmem],
        out_specs=[vmem, vmem, vmem, vmem, hbm, hbm, hbm],
        out_shape=[
            jax.ShapeDtypeStruct(atom_cot.shape, BF16),
            jax.ShapeDtypeStruct((1, experts), F32),
            jax.ShapeDtypeStruct((2, slots, q), BF16),
            jax.ShapeDtypeStruct((32 * experts, 32 * DP), BF16),
            jax.ShapeDtypeStruct((DP, 2 * rows, q), BF16),
            jax.ShapeDtypeStruct((2, 4, 2, rows, q), BF16),
            jax.ShapeDtypeStruct(cots, BF16),
        ],
        scratch_shapes=[
            pltpu.VMEM(edge_feats.shape, BF16),
            pltpu.VMEM((width // LANES, experts, 2 * rows, LANES), BF16),
            pltpu.VMEM((2 * rows, width), BF16),
            pltpu.VMEM((SLICES, 16, COLS), BF16),
            pltpu.VMEM((2, 4, 2, 16, width), BF16),
            pltpu.VMEM(cots, BF16),
            pltpu.VMEM((DP, rows, q), BF16),
            pltpu.VMEM((DP, 2 * rows, q), BF16),
            pltpu.VMEM((2, 4, 2, rows, q), BF16),
            pltpu.VMEM((MP, 1, LANES), F32),
            pltpu.VMEM((2, 2 * rows, LANES), F32),
            *sums,
            dma(()), dma((width // LANES,)), dma((14,)), dma((COPIES,)), dma((COPIES,)),
        ],
        compiler_params=pltpu.CompilerParams(
            collective_id=0, has_side_effects=True, vmem_limit_bytes=56 * 2**20
        ),
        cost_estimate=pl.CostEstimate(flops=4 * 10**9, bytes_accessed=2 * 10**7, transcendentals=0),
    )(
        edge_feats, targets[None], roll_ids[None], counts, coefs, weights, roll_angles[None], atom_cot
    )


def mix_kernel(norm, left_ref, both_ref, cot_ref, back_ref, spread_ref, wg_hbm, eg_ref, gm_ref, out_ref, sem):
    step, steps = pl.program_id(0), pl.num_programs(0)
    crystals, double, _ = both_ref.shape
    experts, _, _, width = wg_hbm.shape
    wg_rows = wg_hbm.reshape(experts, double, width)

    for i in range(crystals):
        cot = jnp.concatenate(
            [cot_ref[0, i // 2, i % 2 + 2 * h].reshape(LANES, COLS) for h in range(2)], 0
        )
        gm_ref[i] = (dot(both_ref[i], cot, ((1,), (0,))) * norm).astype(BF16)

    slot = lax.rem(step, 2)

    def copies(step):
        slot = lax.rem(step, 2)
        return [
            pltpu.make_async_copy(
                out_ref.at[slot, t],
                wg_rows.at[:, :, pl.ds(pl.multiple_of(step * COLS + t * LANES, LANES), LANES)],
                sem.at[slot, t],
            )
            for t in range(2)
        ]

    @pl.when(step >= 2)
    def _():
        for copy in copies(step - 2):
            copy.wait()

    for g in range(double // 32):
        right = jnp.concatenate([gm_ref[i, g * 32 : (g + 1) * 32, :] for i in range(crystals)], 0)
        out = dot(left_ref[...], right, ((1,), (0,))).astype(BF16)
        for t in range(2):
            for k in range(experts):
                piece = out[k * 32 : (k + 1) * 32, t * LANES : (t + 1) * LANES]
                out_ref[slot, t, k, g * 32 : (g + 1) * 32] = piece

    for copy in copies(step):
        copy.start()

    part = step // (steps // 2)
    cols = eg_ref.shape[1]
    at = pl.multiple_of(step % (steps // 2) * cols, cols)
    eg_ref[...] = dot(spread_ref[part], back_ref[pl.ds(at, cols), :], ((1,), (1,))).astype(BF16)

    @pl.when(step == steps - 1)
    def _():
        for copy in copies(step - 1) + copies(step):
            copy.wait()


def mix(experts, left, both_all, cot_all, back_all, spread, norm):
    crystals, double, _ = both_all.shape
    width = back_all.shape[0]
    slots = spread.shape[1]
    whole = lambda shape: pl.BlockSpec(shape, lambda i: (0,) * len(shape))
    return pl.pallas_call(
        functools.partial(mix_kernel, norm),
        grid=(SLICES,),
        in_specs=[
            whole(left.shape),
            whole(both_all.shape),
            pl.BlockSpec((1,) + cot_all.shape[1:], lambda i: (i,) + (0,) * 6),
            whole(back_all.shape),
            whole(spread.shape),
        ],
        out_specs=[
            pl.BlockSpec(memory_space=pl.ANY),
            pl.BlockSpec((slots, 2 * width // SLICES), lambda i: (0, i)),
        ],
        out_shape=[
            jax.ShapeDtypeStruct((experts, double // 2, 2, width), BF16),
            jax.ShapeDtypeStruct((slots, 2 * width), BF16),
        ],
        scratch_shapes=[
            pltpu.VMEM((crystals, double, COLS), BF16),
            pltpu.VMEM((2, 2, experts, double, LANES), BF16),
            pltpu.SemaphoreType.DMA((2, 2)),
        ],
        compiler_params=pltpu.CompilerParams(vmem_limit_bytes=60 * 2**20),
        cost_estimate=pl.CostEstimate(flops=10**10, bytes_accessed=2 * 10**7, transcendentals=0),
    )(left, both_all, cot_all, back_all, spread)


def on_device(edge_feats, targets, roll_ids, counts, coefs, weights, roll_angles, atom_cot):
    slots = edge_feats.shape[0]
    atom_out, coef_grad, spread, left, both_all, back_all, cot_all = exchange(
        edge_feats, targets, roll_ids, counts, coefs, weights, roll_angles, atom_cot
    )
    back_all = back_all.reshape(-1, back_all.shape[-1])
    weight_grad, edge_grad = mix(
        weights.shape[0], left, both_all, cot_all, back_all, spread, (slots * MP) ** -0.5
    )
    return (atom_out, edge_grad, weight_grad, coef_grad)


def solution(mesh):
    placed = (
        P(("dp", "mp"), None),
        P(("dp", "mp")),
        P(("dp", "mp")),
        P(("dp", "mp")),
        P(),
        P(None, "mp", None, None),
        P(),
        P(("dp", "mp"), None),
    )
    return jax.shard_map(
        on_device,
        mesh=mesh,
        in_specs=placed,
        out_specs=(
            P(("dp", "mp"), None),
            P(("dp", "mp"), None),
            P(None, "mp", None, None),
            P("dp", None),
        ),
        check_vma=False,
    )
```

```python
import functools

import jax
import jax.numpy as jnp
from jax import lax
from jax.experimental import pallas as pl
from jax.experimental.pallas import tpu as pltpu
from jax.sharding import PartitionSpec as P

BF16, F32 = jnp.bfloat16, jnp.float32
LANES = 128
MESH = pl.DeviceIdType.MESH
DP, MP = 8, 16
SLICES, COLS = 6, 256
FLOWS = ((0, "xyz"), (1, "zxy"), (2, "yzx"))
SWAP, RING, PLANE, X_SUM, OUT_SUM, COT, BACK, X_DP, COEF = 0, 1, 28, 40, 48, 56, 64, 72, 76
RELAY = COEF + MP - 1
COPIES = RELAY + 6


def dot(a, b, contract):
    return lax.dot_general(a, b, (contract, ((), ())), preferred_element_type=F32)


def turn(rows):
    n = rows.shape[1]
    col = lax.broadcasted_iota(jnp.int32, rows.shape, 1)
    return jnp.where(col // 8 % 2 == 0, pltpu.roll(rows, n - 8, 1), -pltpu.roll(rows, 8, 1))


def interleave(wide, even, odd):
    n = even.shape[0]
    for h in range(2):
        wide[h, pl.ds(0, n, stride=2), :] = even[:, h * LANES : (h + 1) * LANES]
        wide[h, pl.ds(1, n, stride=2), :] = odd[:, h * LANES : (h + 1) * LANES]
    return jnp.concatenate([wide[0], wide[1]], 1)


def separate(wide, both):
    n = both.shape[0] // 2
    for h in range(2):
        wide[h] = both[:, h * LANES : (h + 1) * LANES]
    return [
        jnp.concatenate([wide[h, pl.ds(part, n, stride=2), :] for h in range(2)], 1) for part in range(2)
    ]


def remote(src, dst, send, recv, target):
    return pltpu.make_async_remote_copy(
        src_ref=src, dst_ref=dst, send_sem=send, recv_sem=recv, device_id=target, device_id_type=MESH
    )


def column_of(row):
    n = row.shape[1]
    same = lax.broadcasted_iota(jnp.int32, (n, n), 0) == lax.broadcasted_iota(jnp.int32, (n, n), 1)
    return jnp.sum(jnp.where(same, row, 0.0), 1, keepdims=True)


def exchange_kernel(
    scale, norm,
    feats_hbm, targets_ref, rolls_ref, counts_ref, coefs_ref, weights_hbm, angles_ref, cot_ref,
    atom_ref, coef_ref, spread_ref, left_ref, both_hbm, back_hbm, cot_hbm,
    feats, weights, merged, mine, crystal, cots, x_all, both_all, back_all, coef_parts, wide,
    x_parts, x_pair, x_held, x_slots, x_cross, out_parts, out_pair, out_held, out_slots, out_cross,
    load_sem, weight_sem, store_sem, send_sem, recv_sem,
):
    d, m = lax.axis_index("dp"), lax.axis_index("mp")
    z, y, x, core = d // 2, m // 8 * 2 + d % 2, m // 2 % 4, m % 2
    y_hi, y_lo = m // 8, d % 2
    tiles, experts, double, _ = weights.shape
    rows, width = double // 2, tiles * LANES
    other = 1 - core
    ahead, behind, far = (x + 1) % 4, (x + 3) % 4, (x + 2) % 4

    def device(z, y, x, core):
        return (z * 2 + y % 2, y // 2 * 8 + x * 2 + core)

    sibling = device(z, y, x, other)
    x_next, x_last = device(z, y, ahead, core), device(z, y, behind, core)
    y_peer = device(z, (y + 2) % 4, x, core)
    x_far, z_far = device(z, y, far, core), device((z + 2) % 4, y, x, core)
    z_next, z_last = device((z + 1) % 4, y, x, core), device((z + 3) % 4, y, x, core)
    y_next, y_last = device(z, (y + 1) % 4, x, core), device(z, (y + 3) % 4, x, core)
    lo_peer = (d + 1 - 2 * y_lo, m)

    def mp_peer(j):
        return (d, lax.rem(m + j, MP))

    def span(start, stop, body):
        lax.fori_loop(start, stop, lambda j, c: (body(j), c)[1], 0)

    barrier = pltpu.get_barrier_semaphore()
    span(1, MP, lambda j: pl.semaphore_signal(barrier, inc=1, device_id=mp_peer(j), device_id_type=MESH))
    for to in (z_next, z_last, z_far, y_next, y_last):
        pl.semaphore_signal(barrier, inc=1, device_id=to, device_id_type=MESH)

    feats_copy = pltpu.make_async_copy(feats_hbm, feats, load_sem)
    feats_copy.start()
    weight_rows = weights_hbm.reshape(experts, double, width)

    def weight_copy(t):
        cols = pl.ds(pl.multiple_of(t * LANES, LANES), LANES)
        return pltpu.make_async_copy(weight_rows.at[:, :, cols], weights.at[t], weight_sem.at[t])

    span(0, tiles, lambda t: weight_copy(t).start())

    sent = []

    def send(sem, src, dst, to):
        copy = remote(src, dst, send_sem.at[sem], recv_sem.at[sem], to)
        copy.start()
        sent.append(copy)

    def arrive(sem, ref):
        remote(ref, ref, send_sem.at[sem], recv_sem.at[sem], sibling).wait_recv()

    c = cot_ref[...].astype(F32)
    own = jnp.concatenate([c[:, :width], c[:, width:]], 0).astype(BF16)
    crystal[y_hi, x, core] = own
    for s in range(SLICES):
        mine[s] = own[:, s * COLS : (s + 1) * COLS]
    for o in range(3):
        cots[3 * core + o, z, y, x, core] = mine[3 * core + o]

    slots = targets_ref.shape[1]
    table = rolls_ref[...] == lax.broadcasted_iota(jnp.int32, (angles_ref.shape[1], slots), 0)
    angle = column_of(angles_ref[...])
    valid = lax.broadcasted_iota(jnp.int32, (1, slots), 1) < counts_ref[0]
    factor = jnp.where(valid, scale, 0.0)
    cosine = column_of(jnp.sum(jnp.where(table, jnp.cos(angle), 0.0), 0, keepdims=True) * factor)
    sine = column_of(jnp.sum(jnp.where(table, jnp.sin(angle), 0.0), 0, keepdims=True) * factor)
    target = column_of(targets_ref[...].astype(F32)).astype(jnp.int32)
    q = lax.broadcasted_iota(jnp.int32, (slots, spread_ref.shape[2]), 1)
    hit = target == q // 16 * 8 + q % 8
    real = q // 8 % 2 == 0
    spread_ref[0] = jnp.where(hit, jnp.where(real, cosine, sine), 0.0).astype(BF16)
    spread_ref[1] = jnp.where(hit, jnp.where(real, -sine, cosine), 0.0).astype(BF16)

    pl.semaphore_wait(barrier, MP - 1 + 5)

    theirs = pl.ds(3 * other, 3)
    send(SWAP, mine.at[theirs], cots.at[theirs, z, y, x, core], sibling)

    here = {"z": z, "y": y, "x": x}
    nexts = {"z": (z_next, z_last, z_far), "y": (y_next, y_last, y_peer), "x": (x_next, x_last, x_far)}

    def region(o, stage, by, whose, ref=cots, half=None):
        order = FLOWS[o][1]
        index = dict(here)
        for a in order[:stage]:
            index[a] = slice(None)
        index[order[stage]] = (here[order[stage]] + by) % 4
        if half is not None:
            index["y" if order[stage] == "z" else "z"] = slice(2 * half, 2 * half + 2)
        return ref.at[3 * whose + o, index["z"], index["y"], index["x"]]

    def ring_send(stage, which=(0, 1, 2), ways=(0, 1, 2)):
        for o in which:
            ref = region(o, stage, 0, core)
            for i in ways:
                send(RING + (o * 3 + stage) * 3 + i, ref, ref, nexts[FLOWS[o][1][stage]][i])

    def ring_arrive(o, stage, i):
        arrive(RING + (o * 3 + stage) * 3 + i, region(o, stage, (3, 1, 2)[i], core))

    def ring_relay(o):
        for h, by in ((0, 3), (1, 1)):
            ring_arrive(o, 2, h)
            ref = region(o, 2, by, core, half=h)
            send(RELAY + 2 * o + h, ref, ref, nexts[FLOWS[o][1][2]][h])
            plane_send(o, by)

    def ring_end(o):
        for h in range(2):
            arrive(RELAY + 2 * o + h, region(o, 2, 2, core, half=h))
        plane_send(o, 2)

    def ring_all(stage):
        for o in range(3):
            for i in range(3):
                ring_arrive(o, stage, i)

    stores = []

    def store(src, dst):
        copy = pltpu.make_async_copy(src, dst, store_sem.at[len(stores)])
        copy.start()
        stores.append(copy)

    def plane_send(o, by):
        src, dst = region(o, 2, by, core), region(o, 2, by, core, cot_hbm)
        send(PLANE + o * 4 + by, src, dst, sibling)
        store(src, dst)

    def plane_arrive(o, by):
        arrive(PLANE + o * 4 + by, region(o, 2, by, other, cot_hbm))

    low = 1 - y_hi
    along = ((x_next, ahead), (x_last, behind), (x_far, far))

    def sum_cores(base, parts, pair):
        send(base, parts.at[other], pair, sibling)

    def sum_x(base, parts, pair, held, slots):
        arrive(base, pair)
        for n, h in enumerate((low, y_hi)):
            for i in range(4):
                held[i, h] = (parts[core, h, i].astype(F32) + pair[h, i].astype(F32)).astype(BF16)
            for i, (to, at) in enumerate(along):
                send(base + 1 + 3 * n + i, held.at[at, h], slots.at[n, i], to)

    def sum_of(base, held, slots, n, h):
        total = held[x, h].astype(F32)
        for i in range(3):
            arrive(base + 1 + 3 * n + i, slots.at[n, i])
            total += slots[n, i].astype(F32)
        return total

    def sum_y(base, held, slots, cross):
        cross[0] = sum_of(base, held, slots, 0, low).astype(BF16)
        send(base + 7, cross.at[0], cross.at[1], y_peer)

    def sum_end(base, held, slots, cross):
        total = sum_of(base, held, slots, 1, y_hi)
        arrive(base + 7, cross.at[1])
        return total + cross[1].astype(F32)

    def gather_first(base, ref):
        own = ref.at[y_hi, x, core]
        for i, to in enumerate((y_peer, x_next, x_last, x_far)):
            send(base + i, own, own, to)

    def gather_second(base, ref):
        got = ref.at[low, x, core]
        arrive(base, got)
        for i, (to, _) in enumerate(along):
            send(base + 4 + i, got, got, to)

    def gather_cores(base, ref):
        for n, h in enumerate((y_hi, low)):
            for i, at in enumerate((behind, ahead, far)):
                arrive(base + 1 + 3 * n + i, ref.at[h, at, core])
        ours = ref.at[:, :, core]
        send(base + 7, ours, ours, sibling)

    def gather_end(base, ref):
        arrive(base + 7, ref.at[:, :, other])

    gather_first(COT, crystal)
    arrive(SWAP, cots.at[pl.ds(3 * core, 3), z, y, x, other])
    ring_send(0)

    feats_copy.wait()
    group = 4
    block = group * rows

    def spread_block(i):
        plus = feats[:, pl.ds(pl.multiple_of(i * block, block), block)]
        minus = feats[:, pl.ds(pl.multiple_of(width + i * block, block), block)]
        part = dot(plus, spread_ref[0], ((0,), (0,))) + dot(minus, spread_ref[1], ((0,), (0,)))
        part = part.astype(BF16)
        for g in range(group):
            x_parts[g % 2, i // 2, i % 2 * 2 + g // 2] = part[g * rows : (g + 1) * rows]

    span(0, width // block, spread_block)
    sum_cores(X_SUM, x_parts, x_pair)
    sum_x(X_SUM, x_parts, x_pair, x_held, x_slots)
    gather_second(COT, crystal)
    ring_all(0)
    ring_send(1)

    def merge(t):
        weight_copy(t).wait()
        total = jnp.zeros((double, LANES), F32)
        for k in range(experts):
            total += coefs_ref[d, k] * weights[t, k].astype(F32)
        merged[:, pl.ds(pl.multiple_of(t * LANES, LANES), LANES)] = total.astype(BF16)

    span(0, 2 * tiles // 3, merge)
    sum_y(X_SUM, x_held, x_slots, x_cross)
    span(2 * tiles // 3, tiles, merge)
    ring_all(1)
    ring_send(2, (0,), (0, 1))
    gather_cores(COT, crystal)
    x_here = sum_end(X_SUM, x_held, x_slots, x_cross).astype(BF16)
    x_all[d] = x_here
    send(X_DP, x_all.at[d], x_all.at[d], lo_peer)
    x_wide = x_here.astype(F32)
    both = interleave(wide, x_wide, -turn(x_wide))
    both_turned = both.T.astype(BF16)
    both = both.astype(BF16)

    def out_block(i):
        cols = pl.ds(pl.multiple_of(i * block, block), block)
        part = dot(both_turned, merged[:, cols], ((1,), (0,))).astype(BF16)
        for p in range(MP):
            out_parts[p % 2, p // 8, p // 2 % 4, :, cols] = part[p * 16 : (p + 1) * 16]

    span(0, width // block, out_block)
    sum_cores(OUT_SUM, out_parts, out_pair)

    gather_end(COT, crystal)
    by_real, by_imag = separate(wide, dot(merged[...], crystal[...].reshape(-1, width), ((1,), (1,))))
    back_all[y_hi, x, core] = (by_real + turn(by_imag)).astype(BF16)
    gather_first(BACK, back_all)
    sum_x(OUT_SUM, out_parts, out_pair, out_held, out_slots)
    ring_send(2, (1,), (0, 1))
    gather_second(BACK, back_all)
    ring_send(2, (2,), (0, 1))
    ring_relay(0)
    for o in range(3):
        plane_send(o, 0)
    pair = x_all.at[pl.ds(2 * z, 2)]
    arrive(X_DP, x_all.at[d + 1 - 2 * y_lo])
    for i, to in enumerate((z_next, z_last, z_far)):
        send(X_DP + 1 + i, pair, pair, to)

    def coef_add(t, sums):
        cols = pl.ds(pl.multiple_of(t * LANES, LANES), LANES)
        grad = dot(both, crystal[:, :, :, :, cols].reshape(-1, LANES), ((1,), (0,))) * norm
        added = []
        for k in range(experts):
            terms = weights[t, k].astype(F32) * grad
            added.append(sums[k] + jnp.sum(terms.reshape(-1, 8, LANES), 0))
        return tuple(added)

    sums = tuple(jnp.zeros((8, LANES), F32) for _ in range(experts))
    sums = lax.fori_loop(0, tiles // 2, coef_add, sums)
    sum_y(OUT_SUM, out_held, out_slots, out_cross)
    ring_relay(1)
    sums = lax.fori_loop(tiles // 2, tiles, coef_add, sums)
    lanes = jnp.sum(jnp.concatenate([jnp.sum(v, 0, keepdims=True) for v in sums], 0), 1, keepdims=True)
    same = lax.broadcasted_iota(jnp.int32, (experts, LANES), 0) == lax.broadcasted_iota(
        jnp.int32, (experts, LANES), 1
    )
    coef_parts[0] = jnp.sum(jnp.where(same, lanes, 0.0), 0, keepdims=True)

    def coef_copy(j):
        sem = COEF + j - 1
        return remote(coef_parts.at[0], coef_parts.at[j], send_sem.at[sem], recv_sem.at[sem], mp_peer(j))

    span(1, MP, lambda j: coef_copy(j).start())

    gather_cores(BACK, back_all)
    ring_relay(2)

    r = lax.broadcasted_iota(jnp.int32, (32, 32 * DP), 0)
    c = lax.broadcasted_iota(jnp.int32, (32, 32 * DP), 1)
    for k in range(experts):
        row = jnp.zeros((32, 32 * DP), F32)
        for i in range(DP):
            row = jnp.where(c == r + 32 * i, coefs_ref[i, k], row)
        left_ref[k * 32 : (k + 1) * 32] = row.astype(BF16)

    out = sum_end(OUT_SUM, out_held, out_slots, out_cross)
    half = out.shape[0] // 2
    atom_ref[...] = jnp.concatenate([out[:half], out[half:]], 1).astype(BF16)

    for by, i in ((3, 0), (1, 1), (2, 2)):
        arrive(X_DP + 1 + i, x_all.at[pl.ds((z + by) % 4 * 2, 2)])
    for i in range(DP):
        rows_of = x_all[i].astype(F32)
        both_all[i] = interleave(wide, rows_of, -turn(rows_of)).astype(BF16)

    store(both_all, both_hbm)
    gather_end(BACK, back_all)
    store(back_all, back_hbm)
    for o in range(3):
        ring_end(o)

    span(1, MP, lambda j: coef_copy(j).wait_recv())
    coef_ref[...] = jnp.sum(coef_parts[...], 0)[:, :experts] * (width**-0.5)

    for by in (0, 3, 1, 2):
        for o in range(3):
            plane_arrive(o, by)

    span(1, MP, lambda j: coef_copy(j).wait_send())
    for copy in sent:
        copy.wait_send()
    for copy in stores:
        copy.wait()


def exchange(edge_feats, targets, roll_ids, counts, coefs, weights, roll_angles, atom_cot):
    slots, wide = edge_feats.shape
    width = wide // 2
    experts, rows = weights.shape[:2]
    atoms_here = atom_cot.shape[0]
    q = 2 * MP * atoms_here
    vmem = pl.BlockSpec(memory_space=pltpu.VMEM)
    smem = pl.BlockSpec(memory_space=pltpu.SMEM)
    hbm = pl.BlockSpec(memory_space=pl.ANY)
    dma = pltpu.SemaphoreType.DMA
    cots = (SLICES, 4, 4, 4, 2, 16, COLS)
    sums = [
        pltpu.VMEM(lead + block, BF16)
        for block in ((rows, q), (16, width))
        for lead in ((2, 2, 4), (2, 4), (4, 2), (2, 3), (2,))
    ]
    return pl.pallas_call(
        functools.partial(exchange_kernel, (atoms_here / slots) ** 0.5, (slots * MP) ** -0.5),
        in_specs=[hbm, vmem, vmem, smem, smem, hbm, vmem, vmem],
        out_specs=[vmem, vmem, vmem, vmem, hbm, hbm, hbm],
        out_shape=[
            jax.ShapeDtypeStruct(atom_cot.shape, BF16),
            jax.ShapeDtypeStruct((1, experts), F32),
            jax.ShapeDtypeStruct((2, slots, q), BF16),
            jax.ShapeDtypeStruct((32 * experts, 32 * DP), BF16),
            jax.ShapeDtypeStruct((DP, 2 * rows, q), BF16),
            jax.ShapeDtypeStruct((2, 4, 2, rows, q), BF16),
            jax.ShapeDtypeStruct(cots, BF16),
        ],
        scratch_shapes=[
            pltpu.VMEM(edge_feats.shape, BF16),
            pltpu.VMEM((width // LANES, experts, 2 * rows, LANES), BF16),
            pltpu.VMEM((2 * rows, width), BF16),
            pltpu.VMEM((SLICES, 16, COLS), BF16),
            pltpu.VMEM((2, 4, 2, 16, width), BF16),
            pltpu.VMEM(cots, BF16),
            pltpu.VMEM((DP, rows, q), BF16),
            pltpu.VMEM((DP, 2 * rows, q), BF16),
            pltpu.VMEM((2, 4, 2, rows, q), BF16),
            pltpu.VMEM((MP, 1, LANES), F32),
            pltpu.VMEM((2, 2 * rows, LANES), F32),
            *sums,
            dma(()), dma((width // LANES,)), dma((14,)), dma((COPIES,)), dma((COPIES,)),
        ],
        compiler_params=pltpu.CompilerParams(
            collective_id=0, has_side_effects=True, vmem_limit_bytes=56 * 2**20
        ),
        cost_estimate=pl.CostEstimate(flops=4 * 10**9, bytes_accessed=2 * 10**7, transcendentals=0),
    )(
        edge_feats, targets[None], roll_ids[None], counts, coefs, weights, roll_angles[None], atom_cot
    )


def mix_kernel(norm, left_ref, both_ref, cot_ref, back_ref, spread_ref, wg_hbm, eg_ref, gm_ref, out_ref, sem):
    step, steps = pl.program_id(0), pl.num_programs(0)
    crystals, double, _ = both_ref.shape
    experts, _, _, width = wg_hbm.shape
    wg_rows = wg_hbm.reshape(experts, double, width)

    for i in range(crystals):
        cot = jnp.concatenate(
            [cot_ref[0, i // 2, i % 2 + 2 * h].reshape(LANES, COLS) for h in range(2)], 0
        )
        gm_ref[i] = (dot(both_ref[i], cot, ((1,), (0,))) * norm).astype(BF16)

    slot = lax.rem(step, 2)

    def copies(step):
        slot = lax.rem(step, 2)
        return [
            pltpu.make_async_copy(
                out_ref.at[slot, t],
                wg_rows.at[:, :, pl.ds(pl.multiple_of(step * COLS + t * LANES, LANES), LANES)],
                sem.at[slot, t],
            )
            for t in range(2)
        ]

    @pl.when(step >= 2)
    def _():
        for copy in copies(step - 2):
            copy.wait()

    for g in range(double // 32):
        right = jnp.concatenate([gm_ref[i, g * 32 : (g + 1) * 32, :] for i in range(crystals)], 0)
        out = dot(left_ref[...], right, ((1,), (0,))).astype(BF16)
        for t in range(2):
            for k in range(experts):
                piece = out[k * 32 : (k + 1) * 32, t * LANES : (t + 1) * LANES]
                out_ref[slot, t, k, g * 32 : (g + 1) * 32] = piece

    for copy in copies(step):
        copy.start()

    part = step // (steps // 2)
    cols = eg_ref.shape[1]
    at = pl.multiple_of(step % (steps // 2) * cols, cols)
    eg_ref[...] = dot(spread_ref[part], back_ref[pl.ds(at, cols), :], ((1,), (1,))).astype(BF16)

    @pl.when(step == steps - 1)
    def _():
        for copy in copies(step - 1) + copies(step):
            copy.wait()


def mix(experts, left, both_all, cot_all, back_all, spread, norm):
    crystals, double, _ = both_all.shape
    width = back_all.shape[0]
    slots = spread.shape[1]
    whole = lambda shape: pl.BlockSpec(shape, lambda i: (0,) * len(shape))
    return pl.pallas_call(
        functools.partial(mix_kernel, norm),
        grid=(SLICES,),
        in_specs=[
            whole(left.shape),
            whole(both_all.shape),
            pl.BlockSpec((1,) + cot_all.shape[1:], lambda i: (i,) + (0,) * 6),
            whole(back_all.shape),
            whole(spread.shape),
        ],
        out_specs=[
            pl.BlockSpec(memory_space=pl.ANY),
            pl.BlockSpec((slots, 2 * width // SLICES), lambda i: (0, i)),
        ],
        out_shape=[
            jax.ShapeDtypeStruct((experts, double // 2, 2, width), BF16),
            jax.ShapeDtypeStruct((slots, 2 * width), BF16),
        ],
        scratch_shapes=[
            pltpu.VMEM((crystals, double, COLS), BF16),
            pltpu.VMEM((2, 2, experts, double, LANES), BF16),
            pltpu.SemaphoreType.DMA((2, 2)),
        ],
        compiler_params=pltpu.CompilerParams(vmem_limit_bytes=60 * 2**20),
        cost_estimate=pl.CostEstimate(flops=10**10, bytes_accessed=2 * 10**7, transcendentals=0),
    )(left, both_all, cot_all, back_all, spread)


def on_device(edge_feats, targets, roll_ids, counts, coefs, weights, roll_angles, atom_cot):
    slots = edge_feats.shape[0]
    atom_out, coef_grad, spread, left, both_all, back_all, cot_all = exchange(
        edge_feats, targets, roll_ids, counts, coefs, weights, roll_angles, atom_cot
    )
    back_all = back_all.reshape(-1, back_all.shape[-1])
    weight_grad, edge_grad = mix(
        weights.shape[0], left, both_all, cot_all, back_all, spread, (slots * MP) ** -0.5
    )
    return (atom_out, edge_grad, weight_grad, coef_grad)


def solution(mesh):
    placed = (
        P(("dp", "mp"), None),
        P(("dp", "mp")),
        P(("dp", "mp")),
        P(("dp", "mp")),
        P(),
        P(None, "mp", None, None),
        P(),
        P(("dp", "mp"), None),
    )
    return jax.shard_map(
        on_device,
        mesh=mesh,
        in_specs=placed,
        out_specs=(
            P(("dp", "mp"), None),
            P(("dp", "mp"), None),
            P(None, "mp", None, None),
            P("dp", None),
        ),
        check_vma=False,
    )
```

```python
import functools

import jax
import jax.numpy as jnp
from jax import lax
from jax.experimental import pallas as pl
from jax.experimental.pallas import tpu as pltpu
from jax.sharding import PartitionSpec as P

BF16, F32 = jnp.bfloat16, jnp.float32
LANES = 128
MESH = pl.DeviceIdType.MESH
DP, MP = 8, 16
SLICES, COLS = 6, 256
FLOWS = ((0, "xyz"), (1, "zxy"), (2, "yzx"))
SWAP, RING, PLANE, X_SUM, OUT_SUM, COT, BACK, X_DP, COEF = 0, 1, 28, 40, 48, 56, 64, 72, 76
RELAY = COEF + MP - 1
COPIES = RELAY + 6


def dot(a, b, contract):
    return lax.dot_general(a, b, (contract, ((), ())), preferred_element_type=F32)


def turn(rows):
    n = rows.shape[1]
    col = lax.broadcasted_iota(jnp.int32, rows.shape, 1)
    return jnp.where(col // 8 % 2 == 0, pltpu.roll(rows, n - 8, 1), -pltpu.roll(rows, 8, 1))


def interleave(wide, even, odd):
    n = even.shape[0]
    for h in range(2):
        wide[h, pl.ds(0, n, stride=2), :] = even[:, h * LANES : (h + 1) * LANES]
        wide[h, pl.ds(1, n, stride=2), :] = odd[:, h * LANES : (h + 1) * LANES]
    return jnp.concatenate([wide[0], wide[1]], 1)


def separate(wide, both):
    n = both.shape[0] // 2
    for h in range(2):
        wide[h] = both[:, h * LANES : (h + 1) * LANES]
    return [
        jnp.concatenate([wide[h, pl.ds(part, n, stride=2), :] for h in range(2)], 1) for part in range(2)
    ]


def remote(src, dst, send, recv, target):
    return pltpu.make_async_remote_copy(
        src_ref=src, dst_ref=dst, send_sem=send, recv_sem=recv, device_id=target, device_id_type=MESH
    )


def column_of(row):
    n = row.shape[1]
    same = lax.broadcasted_iota(jnp.int32, (n, n), 0) == lax.broadcasted_iota(jnp.int32, (n, n), 1)
    return jnp.sum(jnp.where(same, row, 0.0), 1, keepdims=True)


def exchange_kernel(
    scale, norm,
    feats_hbm, targets_ref, rolls_ref, counts_ref, coefs_ref, weights_hbm, angles_ref, cot_ref,
    atom_ref, coef_ref, spread_ref, left_ref, both_hbm, back_hbm, cot_hbm,
    feats, weights, merged, mine, crystal, cots, x_all, both_all, back_all, coef_parts, wide,
    x_parts, x_pair, x_held, x_slots, x_cross, out_parts, out_pair, out_held, out_slots, out_cross,
    load_sem, weight_sem, store_sem, send_sem, recv_sem,
):
    d, m = lax.axis_index("dp"), lax.axis_index("mp")
    z, y, x, core = d // 2, m // 8 * 2 + d % 2, m // 2 % 4, m % 2
    y_hi, y_lo = m // 8, d % 2
    tiles, experts, double, _ = weights.shape
    rows, width = double // 2, tiles * LANES
    other = 1 - core
    ahead, behind, far = (x + 1) % 4, (x + 3) % 4, (x + 2) % 4

    def device(z, y, x, core):
        return (z * 2 + y % 2, y // 2 * 8 + x * 2 + core)

    sibling = device(z, y, x, other)
    x_next, x_last = device(z, y, ahead, core), device(z, y, behind, core)
    y_peer = device(z, (y + 2) % 4, x, core)
    x_far, z_far = device(z, y, far, core), device((z + 2) % 4, y, x, core)
    z_next, z_last = device((z + 1) % 4, y, x, core), device((z + 3) % 4, y, x, core)
    y_next, y_last = device(z, (y + 1) % 4, x, core), device(z, (y + 3) % 4, x, core)
    lo_peer = (d + 1 - 2 * y_lo, m)

    def mp_peer(j):
        return (d, lax.rem(m + j, MP))

    def span(start, stop, body):
        lax.fori_loop(start, stop, lambda j, c: (body(j), c)[1], 0)

    barrier = pltpu.get_barrier_semaphore()
    span(1, MP, lambda j: pl.semaphore_signal(barrier, inc=1, device_id=mp_peer(j), device_id_type=MESH))
    for to in (z_next, z_last, z_far, y_next, y_last):
        pl.semaphore_signal(barrier, inc=1, device_id=to, device_id_type=MESH)

    feats_copy = pltpu.make_async_copy(feats_hbm, feats, load_sem)
    feats_copy.start()
    weight_rows = weights_hbm.reshape(experts, double, width)

    def weight_copy(t):
        cols = pl.ds(pl.multiple_of(t * LANES, LANES), LANES)
        return pltpu.make_async_copy(weight_rows.at[:, :, cols], weights.at[t], weight_sem.at[t])

    span(0, tiles, lambda t: weight_copy(t).start())

    sent = []

    def send(sem, src, dst, to):
        copy = remote(src, dst, send_sem.at[sem], recv_sem.at[sem], to)
        copy.start()
        sent.append(copy)

    def arrive(sem, ref):
        remote(ref, ref, send_sem.at[sem], recv_sem.at[sem], sibling).wait_recv()

    c = cot_ref[...].astype(F32)
    own = jnp.concatenate([c[:, :width], c[:, width:]], 0).astype(BF16)
    crystal[y_hi, x, core] = own
    for s in range(SLICES):
        mine[s] = own[:, s * COLS : (s + 1) * COLS]
    for o in range(3):
        cots[3 * core + o, z, y, x, core] = mine[3 * core + o]

    slots = targets_ref.shape[1]
    table = rolls_ref[...] == lax.broadcasted_iota(jnp.int32, (angles_ref.shape[1], slots), 0)
    angle = column_of(angles_ref[...])
    valid = lax.broadcasted_iota(jnp.int32, (1, slots), 1) < counts_ref[0]
    factor = jnp.where(valid, scale, 0.0)
    cosine = column_of(jnp.sum(jnp.where(table, jnp.cos(angle), 0.0), 0, keepdims=True) * factor)
    sine = column_of(jnp.sum(jnp.where(table, jnp.sin(angle), 0.0), 0, keepdims=True) * factor)
    target = column_of(targets_ref[...].astype(F32)).astype(jnp.int32)
    q = lax.broadcasted_iota(jnp.int32, (slots, spread_ref.shape[2]), 1)
    hit = target == q // 16 * 8 + q % 8
    real = q // 8 % 2 == 0
    spread_ref[0] = jnp.where(hit, jnp.where(real, cosine, sine), 0.0).astype(BF16)
    spread_ref[1] = jnp.where(hit, jnp.where(real, -sine, cosine), 0.0).astype(BF16)

    pl.semaphore_wait(barrier, MP - 1 + 5)

    theirs = pl.ds(3 * other, 3)
    send(SWAP, mine.at[theirs], cots.at[theirs, z, y, x, core], sibling)

    here = {"z": z, "y": y, "x": x}
    nexts = {"z": (z_next, z_last, z_far), "y": (y_next, y_last, y_peer), "x": (x_next, x_last, x_far)}

    def region(o, stage, by, whose, ref=cots, half=None):
        order = FLOWS[o][1]
        index = dict(here)
        for a in order[:stage]:
            index[a] = slice(None)
        index[order[stage]] = (here[order[stage]] + by) % 4
        if half is not None:
            index["y" if order[stage] == "z" else "z"] = slice(2 * half, 2 * half + 2)
        return ref.at[3 * whose + o, index["z"], index["y"], index["x"]]

    def ring_send(stage, which=(0, 1, 2), ways=(0, 1, 2)):
        for o in which:
            ref = region(o, stage, 0, core)
            for i in ways:
                send(RING + (o * 3 + stage) * 3 + i, ref, ref, nexts[FLOWS[o][1][stage]][i])

    def ring_arrive(o, stage, i):
        arrive(RING + (o * 3 + stage) * 3 + i, region(o, stage, (3, 1, 2)[i], core))

    def ring_relay(o):
        for h, by in ((0, 3), (1, 1)):
            ring_arrive(o, 2, h)
            ref = region(o, 2, by, core, half=h)
            send(RELAY + 2 * o + h, ref, ref, nexts[FLOWS[o][1][2]][h])
            plane_send(o, by)

    def ring_end(o):
        for h in range(2):
            arrive(RELAY + 2 * o + h, region(o, 2, 2, core, half=h))
        plane_send(o, 2)

    def ring_all(stage):
        for o in range(3):
            for i in range(3):
                ring_arrive(o, stage, i)

    stores = []

    def store(src, dst):
        copy = pltpu.make_async_copy(src, dst, store_sem.at[len(stores)])
        copy.start()
        stores.append(copy)

    def plane_send(o, by):
        src, dst = region(o, 2, by, core), region(o, 2, by, core, cot_hbm)
        send(PLANE + o * 4 + by, src, dst, sibling)
        store(src, dst)

    def plane_arrive(o, by):
        arrive(PLANE + o * 4 + by, region(o, 2, by, other, cot_hbm))

    low = 1 - y_hi
    along = ((x_next, ahead), (x_last, behind), (x_far, far))

    def sum_cores(base, parts, pair):
        send(base, parts.at[other], pair, sibling)

    def sum_x(base, parts, pair, held, slots):
        arrive(base, pair)
        for n, h in enumerate((low, y_hi)):
            for i in range(4):
                held[i, h] = (parts[core, h, i].astype(F32) + pair[h, i].astype(F32)).astype(BF16)
            for i, (to, at) in enumerate(along):
                send(base + 1 + 3 * n + i, held.at[at, h], slots.at[n, i], to)

    def sum_of(base, held, slots, n, h):
        total = held[x, h].astype(F32)
        for i in range(3):
            arrive(base + 1 + 3 * n + i, slots.at[n, i])
            total += slots[n, i].astype(F32)
        return total

    def sum_y(base, held, slots, cross):
        cross[0] = sum_of(base, held, slots, 0, low).astype(BF16)
        send(base + 7, cross.at[0], cross.at[1], y_peer)

    def sum_end(base, held, slots, cross):
        total = sum_of(base, held, slots, 1, y_hi)
        arrive(base + 7, cross.at[1])
        return total + cross[1].astype(F32)

    def gather_first(base, ref):
        own = ref.at[y_hi, x, core]
        for i, to in enumerate((y_peer, x_next, x_last, x_far)):
            send(base + i, own, own, to)

    def gather_second(base, ref):
        got = ref.at[low, x, core]
        arrive(base, got)
        for i, (to, _) in enumerate(along):
            send(base + 4 + i, got, got, to)

    def gather_cores(base, ref):
        for n, h in enumerate((y_hi, low)):
            for i, at in enumerate((behind, ahead, far)):
                arrive(base + 1 + 3 * n + i, ref.at[h, at, core])
        ours = ref.at[:, :, core]
        send(base + 7, ours, ours, sibling)

    def gather_end(base, ref):
        arrive(base + 7, ref.at[:, :, other])

    gather_first(COT, crystal)
    arrive(SWAP, cots.at[pl.ds(3 * core, 3), z, y, x, other])
    ring_send(0)

    feats_copy.wait()
    group = 4
    block = group * rows

    def spread_block(i):
        plus = feats[:, pl.ds(pl.multiple_of(i * block, block), block)]
        minus = feats[:, pl.ds(pl.multiple_of(width + i * block, block), block)]
        part = dot(plus, spread_ref[0], ((0,), (0,))) + dot(minus, spread_ref[1], ((0,), (0,)))
        part = part.astype(BF16)
        for g in range(group):
            x_parts[g % 2, i // 2, i % 2 * 2 + g // 2] = part[g * rows : (g + 1) * rows]

    span(0, width // block, spread_block)
    sum_cores(X_SUM, x_parts, x_pair)
    sum_x(X_SUM, x_parts, x_pair, x_held, x_slots)
    gather_second(COT, crystal)
    ring_all(0)
    ring_send(1)

    def merge(t):
        weight_copy(t).wait()
        total = jnp.zeros((double, LANES), F32)
        for k in range(experts):
            total += coefs_ref[d, k] * weights[t, k].astype(F32)
        merged[:, pl.ds(pl.multiple_of(t * LANES, LANES), LANES)] = total.astype(BF16)

    span(0, 2 * tiles // 3, merge)
    sum_y(X_SUM, x_held, x_slots, x_cross)
    span(2 * tiles // 3, tiles, merge)
    ring_all(1)
    ring_send(2, (0,), (0, 1))
    gather_cores(COT, crystal)
    x_here = sum_end(X_SUM, x_held, x_slots, x_cross).astype(BF16)
    x_all[d] = x_here
    send(X_DP, x_all.at[d], x_all.at[d], lo_peer)
    x_wide = x_here.astype(F32)
    both = interleave(wide, x_wide, -turn(x_wide))
    both_turned = both.T.astype(BF16)
    both = both.astype(BF16)

    def out_block(i):
        cols = pl.ds(pl.multiple_of(i * block, block), block)
        part = dot(both_turned, merged[:, cols], ((1,), (0,))).astype(BF16)
        for p in range(MP):
            out_parts[p % 2, p // 8, p // 2 % 4, :, cols] = part[p * 16 : (p + 1) * 16]

    span(0, width // block, out_block)
    sum_cores(OUT_SUM, out_parts, out_pair)

    gather_end(COT, crystal)
    by_real, by_imag = separate(wide, dot(merged[...], crystal[...].reshape(-1, width), ((1,), (1,))))
    back_all[y_hi, x, core] = (by_real + turn(by_imag)).astype(BF16)
    gather_first(BACK, back_all)
    sum_x(OUT_SUM, out_parts, out_pair, out_held, out_slots)
    ring_send(2, (1,), (0, 1))
    gather_second(BACK, back_all)
    ring_send(2, (2,), (0, 1))
    ring_relay(0)
    for o in range(3):
        plane_send(o, 0)
    pair = x_all.at[pl.ds(2 * z, 2)]
    arrive(X_DP, x_all.at[d + 1 - 2 * y_lo])
    for i, to in enumerate((z_next, z_last, z_far)):
        send(X_DP + 1 + i, pair, pair, to)

    def coef_add(t, sums):
        cols = pl.ds(pl.multiple_of(t * LANES, LANES), LANES)
        grad = dot(both, crystal[:, :, :, :, cols].reshape(-1, LANES), ((1,), (0,))) * norm
        added = []
        for k in range(experts):
            terms = weights[t, k].astype(F32) * grad
            added.append(sums[k] + jnp.sum(terms.reshape(-1, 8, LANES), 0))
        return tuple(added)

    sums = tuple(jnp.zeros((8, LANES), F32) for _ in range(experts))
    sums = lax.fori_loop(0, tiles // 2, coef_add, sums)
    sum_y(OUT_SUM, out_held, out_slots, out_cross)
    ring_relay(1)
    sums = lax.fori_loop(tiles // 2, tiles, coef_add, sums)
    lanes = jnp.sum(jnp.concatenate([jnp.sum(v, 0, keepdims=True) for v in sums], 0), 1, keepdims=True)
    same = lax.broadcasted_iota(jnp.int32, (experts, LANES), 0) == lax.broadcasted_iota(
        jnp.int32, (experts, LANES), 1
    )
    coef_parts[0] = jnp.sum(jnp.where(same, lanes, 0.0), 0, keepdims=True)

    def coef_copy(j):
        sem = COEF + j - 1
        return remote(coef_parts.at[0], coef_parts.at[j], send_sem.at[sem], recv_sem.at[sem], mp_peer(j))

    span(1, MP, lambda j: coef_copy(j).start())

    gather_cores(BACK, back_all)
    ring_relay(2)

    r = lax.broadcasted_iota(jnp.int32, (32, 32 * DP), 0)
    c = lax.broadcasted_iota(jnp.int32, (32, 32 * DP), 1)
    for k in range(experts):
        row = jnp.zeros((32, 32 * DP), F32)
        for i in range(DP):
            row = jnp.where(c == r + 32 * i, coefs_ref[i, k], row)
        left_ref[k * 32 : (k + 1) * 32] = row.astype(BF16)

    out = sum_end(OUT_SUM, out_held, out_slots, out_cross)
    half = out.shape[0] // 2
    atom_ref[...] = jnp.concatenate([out[:half], out[half:]], 1).astype(BF16)

    for by, i in ((3, 0), (1, 1), (2, 2)):
        arrive(X_DP + 1 + i, x_all.at[pl.ds((z + by) % 4 * 2, 2)])
    for i in range(DP):
        rows_of = x_all[i].astype(F32)
        both_all[i] = interleave(wide, rows_of, -turn(rows_of)).astype(BF16)

    store(both_all, both_hbm)
    gather_end(BACK, back_all)
    store(back_all, back_hbm)
    for o in range(3):
        ring_end(o)

    span(1, MP, lambda j: coef_copy(j).wait_recv())
    coef_ref[...] = jnp.sum(coef_parts[...], 0)[:, :experts] * (width**-0.5)

    for by in (0, 3, 1, 2):
        for o in range(3):
            plane_arrive(o, by)

    span(1, MP, lambda j: coef_copy(j).wait_send())
    for copy in sent:
        copy.wait_send()
    for copy in stores:
        copy.wait()


def exchange(edge_feats, targets, roll_ids, counts, coefs, weights, roll_angles, atom_cot):
    slots, wide = edge_feats.shape
    width = wide // 2
    experts, rows = weights.shape[:2]
    atoms_here = atom_cot.shape[0]
    q = 2 * MP * atoms_here
    vmem = pl.BlockSpec(memory_space=pltpu.VMEM)
    smem = pl.BlockSpec(memory_space=pltpu.SMEM)
    hbm = pl.BlockSpec(memory_space=pl.ANY)
    dma = pltpu.SemaphoreType.DMA
    cots = (SLICES, 4, 4, 4, 2, 16, COLS)
    sums = [
        pltpu.VMEM(lead + block, BF16)
        for block in ((rows, q), (16, width))
        for lead in ((2, 2, 4), (2, 4), (4, 2), (2, 3), (2,))
    ]
    return pl.pallas_call(
        functools.partial(exchange_kernel, (atoms_here / slots) ** 0.5, (slots * MP) ** -0.5),
        in_specs=[hbm, vmem, vmem, smem, smem, hbm, vmem, vmem],
        out_specs=[vmem, vmem, vmem, vmem, hbm, hbm, hbm],
        out_shape=[
            jax.ShapeDtypeStruct(atom_cot.shape, BF16),
            jax.ShapeDtypeStruct((1, experts), F32),
            jax.ShapeDtypeStruct((2, slots, q), BF16),
            jax.ShapeDtypeStruct((32 * experts, 32 * DP), BF16),
            jax.ShapeDtypeStruct((DP, 2 * rows, q), BF16),
            jax.ShapeDtypeStruct((2, 4, 2, rows, q), BF16),
            jax.ShapeDtypeStruct(cots, BF16),
        ],
        scratch_shapes=[
            pltpu.VMEM(edge_feats.shape, BF16),
            pltpu.VMEM((width // LANES, experts, 2 * rows, LANES), BF16),
            pltpu.VMEM((2 * rows, width), BF16),
            pltpu.VMEM((SLICES, 16, COLS), BF16),
            pltpu.VMEM((2, 4, 2, 16, width), BF16),
            pltpu.VMEM(cots, BF16),
            pltpu.VMEM((DP, rows, q), BF16),
            pltpu.VMEM((DP, 2 * rows, q), BF16),
            pltpu.VMEM((2, 4, 2, rows, q), BF16),
            pltpu.VMEM((MP, 1, LANES), F32),
            pltpu.VMEM((2, 2 * rows, LANES), F32),
            *sums,
            dma(()), dma((width // LANES,)), dma((14,)), dma((COPIES,)), dma((COPIES,)),
        ],
        compiler_params=pltpu.CompilerParams(
            collective_id=0, has_side_effects=True, vmem_limit_bytes=56 * 2**20
        ),
        cost_estimate=pl.CostEstimate(flops=4 * 10**9, bytes_accessed=2 * 10**7, transcendentals=0),
    )(
        edge_feats, targets[None], roll_ids[None], counts, coefs, weights, roll_angles[None], atom_cot
    )


def mix_kernel(norm, left_ref, both_ref, cot_ref, back_ref, spread_ref, atom_in, coef_in, wg_hbm, eg_ref, atom_ref,
               coef_ref, gm_ref, out_ref, sem):
    @pl.when(pl.program_id(0) == 0)
    def _():
        atom_ref[...] = atom_in[...]
        coef_ref[...] = coef_in[...]

    step, steps = pl.program_id(0), pl.num_programs(0)
    crystals, double, _ = both_ref.shape
    experts, _, _, width = wg_hbm.shape
    wg_rows = wg_hbm.reshape(experts, double, width)

    for i in range(crystals):
        cot = jnp.concatenate(
            [cot_ref[0, i // 2, i % 2 + 2 * h].reshape(LANES, COLS) for h in range(2)], 0
        )
        gm_ref[i] = (dot(both_ref[i], cot, ((1,), (0,))) * norm).astype(BF16)

    slot = lax.rem(step, 2)

    def copies(step):
        slot = lax.rem(step, 2)
        return [
            pltpu.make_async_copy(
                out_ref.at[slot, t],
                wg_rows.at[:, :, pl.ds(pl.multiple_of(step * COLS + t * LANES, LANES), LANES)],
                sem.at[slot, t],
            )
            for t in range(2)
        ]

    @pl.when(step >= 2)
    def _():
        for copy in copies(step - 2):
            copy.wait()

    for g in range(double // 32):
        right = jnp.concatenate([gm_ref[i, g * 32 : (g + 1) * 32, :] for i in range(crystals)], 0)
        out = dot(left_ref[...], right, ((1,), (0,))).astype(BF16)
        for t in range(2):
            for k in range(experts):
                piece = out[k * 32 : (k + 1) * 32, t * LANES : (t + 1) * LANES]
                out_ref[slot, t, k, g * 32 : (g + 1) * 32] = piece

    for copy in copies(step):
        copy.start()

    part = step // (steps // 2)
    cols = eg_ref.shape[1]
    at = pl.multiple_of(step % (steps // 2) * cols, cols)
    eg_ref[...] = dot(spread_ref[part], back_ref[pl.ds(at, cols), :], ((1,), (1,))).astype(BF16)

    @pl.when(step == steps - 1)
    def _():
        for copy in copies(step - 1) + copies(step):
            copy.wait()


def mix(experts, left, both_all, cot_all, back_all, spread, atom_out, coef_grad, norm):
    crystals, double, _ = both_all.shape
    width = back_all.shape[0]
    slots = spread.shape[1]
    whole = lambda shape: pl.BlockSpec(shape, lambda i: (0,) * len(shape))
    return pl.pallas_call(
        functools.partial(mix_kernel, norm),
        grid=(SLICES,),
        in_specs=[
            whole(left.shape),
            whole(both_all.shape),
            pl.BlockSpec((1,) + cot_all.shape[1:], lambda i: (i,) + (0,) * 6),
            whole(back_all.shape),
            whole(spread.shape),
            whole(atom_out.shape),
            whole(coef_grad.shape),
        ],
        out_specs=[
            pl.BlockSpec(memory_space=pl.ANY),
            pl.BlockSpec((slots, 2 * width // SLICES), lambda i: (0, i)),
            whole(atom_out.shape),
            whole(coef_grad.shape),
        ],
        out_shape=[
            jax.ShapeDtypeStruct((experts, double // 2, 2, width), BF16),
            jax.ShapeDtypeStruct((slots, 2 * width), BF16),
            jax.ShapeDtypeStruct(atom_out.shape, BF16),
            jax.ShapeDtypeStruct(coef_grad.shape, F32),
        ],
        scratch_shapes=[
            pltpu.VMEM((crystals, double, COLS), BF16),
            pltpu.VMEM((2, 2, experts, double, LANES), BF16),
            pltpu.SemaphoreType.DMA((2, 2)),
        ],
        compiler_params=pltpu.CompilerParams(vmem_limit_bytes=60 * 2**20),
        cost_estimate=pl.CostEstimate(flops=10**10, bytes_accessed=2 * 10**7, transcendentals=0),
    )(left, both_all, cot_all, back_all, spread, atom_out, coef_grad)


def on_device(edge_feats, targets, roll_ids, counts, coefs, weights, roll_angles, atom_cot):
    slots = edge_feats.shape[0]
    atom_out, coef_grad, spread, left, both_all, back_all, cot_all = exchange(
        edge_feats, targets, roll_ids, counts, coefs, weights, roll_angles, atom_cot
    )
    back_all = back_all.reshape(-1, back_all.shape[-1])
    weight_grad, edge_grad, atom_out, coef_grad = mix(
        weights.shape[0], left, both_all, cot_all, back_all, spread, atom_out, coef_grad, (slots * MP) ** -0.5
    )
    return (atom_out, edge_grad, weight_grad, coef_grad)


def solution(mesh):
    placed = (
        P(("dp", "mp"), None),
        P(("dp", "mp")),
        P(("dp", "mp")),
        P(("dp", "mp")),
        P(),
        P(None, "mp", None, None),
        P(),
        P(("dp", "mp"), None),
    )
    return jax.shard_map(
        on_device,
        mesh=mesh,
        in_specs=placed,
        out_specs=(
            P(("dp", "mp"), None),
            P(("dp", "mp"), None),
            P(None, "mp", None, None),
            P("dp", None),
        ),
        check_vma=False,
    )
```
